128 devices in a mesh: row: 16 (over z, y_lo, core), col: 8 (over y_hi, x).
Axes of the slice: x: 4, y: 4 (y_hi: 2, y_lo: 2; y = y_hi * 2 + y_lo), z: 4, core: 2. Of those that a mesh axis runs over, the one named last changes fastest.
Arguments:
- x_blocks: bfloat16 [256, 16, 3, 4761], P(('row', 'col')), may hold values from -2 to 2
- x_cols: int32 [256, 16, 3], P(('row', 'col')), may hold values from 0 to 15, all different within a row
Outputs:
- product: float32 [17664, 17664], P('row', 'col')
The draws below stay inside these ranges and needn't reach their ends.
Inputs may be any that keep to these rules, and one draw needn't show every extreme that they name: The 3 entries of x_cols[i, g] are distinct, and every value is named by some entry.
All inputs are finite; a program needn't handle non-finite values.
Results may differ from the reference program's by a relative error of at most 0.0003.
Values may be sent and summed in bfloat16 or wider, within the bound.
A program may use at most 192 MiB of HBM per device.

```python
import jax
import jax.numpy as jnp
from jax import lax

BLK = 69
BB = 16
PG = 3
TICKS = 2
GROUPS = 16
NB = 256


def block_levels(own_key, extent, pieces, smallest, high):
    def one(dim, shards_of):
        steps = jax.random.uniform(jax.random.fold_in(jax.random.fold_in(own_key, 6), dim), (shards_of,), jnp.float32, smallest / len(pieces), high / len(pieces))
        return jnp.repeat(jnp.exp(steps), extent[dim] // shards_of).reshape((-1,) + (1,) * (len(extent) - dim - 1))

    gain = one(*pieces[0])
    for cut in pieces[1:]:
        gain = gain * one(*cut)
    return gain


def choose_distinct(rng, rows, number_of, top, lift):
    sequence = jax.random.permutation(jax.random.fold_in(rng, 1), number_of)
    favour = sequence
    for power in range(3):
        favour = favour * favour // number_of
    favour = favour * lift // number_of
    lots = jax.random.randint(jax.random.fold_in(rng, 2), (rows, number_of), 0, 4096) + favour
    holders = jax.random.permutation(jax.random.fold_in(rng, 3), rows)[jnp.arange(number_of) % rows]
    lots = jnp.where(jnp.arange(rows)[:, None] == holders[None, :], 1 << 14, lots)
    merit = lots * number_of + jnp.arange(number_of)
    return lax.top_k(merit.astype(jnp.int32), top)[1].astype(jnp.int32)


def centred(key, shape, scale, reach, split=(), kind=jnp.bfloat16):
    gain = block_levels(key, shape, split, -0.22, 0.18) if split else 1.0
    values = jax.random.normal(key, shape, jnp.float32) * scale * gain
    return jnp.minimum(jnp.maximum(values, -reach), reach).astype(kind)


def setup_inputs(seed: int = 0) -> dict:
    streams_of = jax.random.split(jax.random.key(seed), 3)
    return {
        "x_blocks": centred(streams_of[0], (NB, GROUPS, PG, BLK * BLK), (PG * 3) ** -0.5, 2.0, ((0, 128),)),
        "x_cols": choose_distinct(streams_of[1], NB * GROUPS, BB, PG, 0).reshape((NB, GROUPS, PG)),
    }


def expand_rows(x_blocks, x_cols):
    rows_here = x_blocks.shape[0]
    marker = (x_cols[..., None] == jnp.arange(BB, dtype=jnp.int32)).astype(jnp.float32)
    blocks = jnp.einsum('ngpl,ngpe->ngle', marker, x_blocks.astype(jnp.float32), precision=lax.Precision.HIGHEST)
    blocks = blocks.reshape(rows_here, GROUPS, BB, BLK, BLK).transpose(0, 3, 1, 2, 4)
    return blocks.reshape(rows_here * BLK, NB * BLK).astype(jnp.bfloat16)


def reference(x_blocks, x_cols):
    width = BB * BLK

    def group_rows(index):
        start = (index * BB).astype(jnp.int32)
        values = lax.dynamic_slice_in_dim(x_blocks, start, BB, 0)
        columns = lax.dynamic_slice_in_dim(x_cols, start, BB, 0)
        return expand_rows(values, columns).reshape(width, GROUPS, width)

    expanded = lax.map(group_rows, jnp.arange(GROUPS, dtype=jnp.int32))

    def one_block(pair):
        upper = pair[0]
        lower = pair[1]
        total = jnp.zeros((width, width), jnp.float32)
        for offset in range(TICKS):
            middle = (upper + lower + offset) % GROUPS
            left_panel = expanded[upper, :, middle, :]
            right_panel = expanded[middle, :, lower, :]
            total = total + jnp.dot(left_panel, right_panel, preferred_element_type=jnp.float32)
        return total

    upper_ids = jnp.repeat(jnp.arange(GROUPS, dtype=jnp.int32), GROUPS)
    lower_ids = jnp.tile(jnp.arange(GROUPS, dtype=jnp.int32), GROUPS)
    pairs = jnp.stack([upper_ids, lower_ids], axis=1)
    result = lax.map(one_block, pairs)
    result = result.reshape(GROUPS, GROUPS, width, width).transpose(0, 2, 1, 3)
    return result.reshape(NB * BLK, NB * BLK)
```

```python
import functools

import jax
import jax.numpy as jnp
from jax import lax
from jax.experimental import pallas as pl
from jax.experimental.pallas import tpu as pltpu
from jax.sharding import PartitionSpec as P

BLK = 69
BB = 16
PG = 3
GROUPS = 16
Q = 8
RR = 9
CHUNK = RR * BLK
ROWS = 2 * PG * Q
LANES = 640
KP = 80
SIZE = BLK * BLK
F32 = jnp.float32
BF16 = jnp.bfloat16
MESH = pl.DeviceIdType.MESH
DMA = pltpu.SemaphoreType.DMA


def lane_ids(rows):
    return lax.broadcasted_iota(jnp.int32, (rows, 128), 1)


def pack_kernel(cols_ref, x_ref, f_ref, scr):
    tiles = (SIZE + 127) // 128

    def group(g, _):
        lane = lane_ids(PG)
        for k2 in range(2):
            flat = x_ref[k2, g].astype(F32)
            parts = []
            for t in range(tiles):
                if t < tiles - 1:
                    parts.append(flat[:, 128 * t : 128 * (t + 1)])
                else:
                    last = flat[:, 128 * t : SIZE]
                    parts.append(
                        jnp.concatenate([last, jnp.zeros((PG, 128 * tiles - SIZE), F32)], axis=1)
                    )
            for q in range(Q):
                for t in range(LANES // 128):
                    a, o = divmod(CHUNK * q + 128 * t, 128)
                    if a >= tiles:
                        piece = jnp.zeros((PG, 128), F32)
                    else:
                        low = parts[a]
                        high = parts[a + 1] if a + 1 < tiles else jnp.zeros((PG, 128), F32)
                        piece = jnp.where(lane >= o, low, high)
                        if o:
                            piece = pltpu.roll(piece, 128 - o, 1)
                    scr[t, pl.ds(k2 * PG * Q + q, PG, stride=Q), :] = piece
        lane = lane_ids(ROWS)
        tail = scr[4]
        tail = jnp.where(lane < CHUNK - 512, tail, 0.0)
        for k2 in range(2):
            for p in range(PG):
                value = cols_ref[k2, g * PG + p].astype(F32)
                tail = jnp.where(lane == CHUNK - 512 + k2 * PG + p, value, tail)
        for t in range(4):
            f_ref[g, :, 128 * t : 128 * (t + 1)] = scr[t].astype(BF16)
        f_ref[g, :, 512:640] = tail.astype(BF16)
        return 0

    lax.fori_loop(0, GROUPS, group, 0)


def pack(x_blocks, x_cols):
    return pl.pallas_call(
        pack_kernel,
        out_shape=jax.ShapeDtypeStruct((GROUPS, ROWS, LANES), BF16),
        in_specs=[
            pl.BlockSpec(memory_space=pltpu.SMEM),
            pl.BlockSpec(memory_space=pltpu.VMEM),
        ],
        out_specs=pl.BlockSpec(memory_space=pltpu.VMEM),
        scratch_shapes=[pltpu.VMEM((LANES // 128, ROWS, 128), F32)],
        compiler_params=pltpu.CompilerParams(vmem_limit_bytes=32 << 20),
        name="pack",
    )(x_cols.reshape(2, GROUPS * PG), x_blocks)

def exchange_kernel(F, RF, LF, RX, LY, sa, ra, sb, rb, so, ro, sl, rl, ss, rs, sp, rp, sf, rf, ls):
    row = lax.axis_index("row")
    col = lax.axis_index("col")
    m, e = row // 2, row % 2
    yh, x = col // 4, col % 4

    def remote(src, dst, send, recv, device):
        return pltpu.make_async_remote_copy(
            src_ref=src, dst_ref=dst, send_sem=send, recv_sem=recv, device_id=device, device_id_type=MESH
        )

    at_x = [(x + d) % 4 for d in range(4)]
    peers = {d: (row, yh * 4 + at_x[d]) for d in (1, 2, 3)}
    across = (row, (1 - yh) * 4 + x)
    sibling = (row + 1 - 2 * e, col)
    columns = (x, x + 4)
    single = [(jnp.where(e == 0, 2 * ((m - C + 16) % 8), 2 * ((m - C + 15) % 8) + 1), C) for C in columns]
    pair = [(jnp.where(e == 1, 2 * ((m - C + 16) % 8), 2 * ((m - C + 15) % 8) + 1), C) for C in columns]
    own = [jnp.logical_and(e == 0, col == 0), jnp.logical_and(e == 1, col == 7)]
    any_own = jnp.logical_or(own[0], own[1])
    sources = [((row + 2 * col + e + k) % 16, h * 4 + x) for k in (0, 1) for h in (0, 1)]

    barrier = pltpu.get_barrier_semaphore()
    for device in (peers[1], peers[2], peers[3], across, sibling):
        pl.semaphore_signal(barrier, 1, device_id=device, device_id_type=MESH)
    for device in single + pair + sources:

        @pl.when(jnp.logical_not(jnp.logical_and(device[0] == row, device[1] == col)))
        def _(device=device):
            pl.semaphore_signal(barrier, 1, device_id=device, device_id_type=MESH)

    pl.semaphore_wait(barrier, 13 - 2 * jnp.where(any_own, 1, 0))

    def groups_at(place, ci):
        return 2 * place + 8 * ci

    def spread(d, ci):
        src = F.at[pl.ds(groups_at(at_x[d], ci), 2)]
        return remote(src, RX.at[ci, d - 1], sa.at[d - 1, ci], ra.at[d - 1, ci], peers[d])

    def cross(t):
        src = F.at[pl.ds((row + 8 * (1 - yh) + t) % 16, 1)]
        return remote(src, LY.at[pl.ds(t, 1)], sb.at[t], rb.at[t], across)

    def left_own(d, t, at):
        src = F.at[pl.ds((row + 2 * (yh * 4 + at_x[d]) + t) % 16, 1)]
        return remote(src, LF.at[at, pl.ds(t, 1)], so.at[d - 1, t], ro.at[d - 1, t], peers[d])

    other = (1 - yh) * 4

    def left_across(d, at):
        return remote(LY.at[pl.ds(2 * at_x[d], 3)], LF.at[at], sl.at[d - 1], rl.at[d - 1], peers[d])

    def from_x(d):
        return yh * 4 + (x + 4 - d) % 4

    def right_src(ci, d):
        if d == 0:
            return F.at[pl.ds(groups_at(x, ci) + e, 1)], F.at[pl.ds(groups_at(x, ci), 2)]
        return RX.at[ci, d - 1, pl.ds(e, 1)], RX.at[ci, d - 1]

    def right_pair(ci, d):
        at = from_x(d)
        return remote(right_src(ci, d)[1], RF.at[pl.ds(1, 2), at], sp.at[ci, d], rp.at[at], pair[ci])

    def right_single(ci, d):
        at = from_x(d)
        return remote(right_src(ci, d)[0], RF.at[pl.ds(3 * e, 1), at], ss.at[ci, d], rs.at[at], single[ci])

    def right_here(ci, d):
        return pltpu.make_async_copy(right_src(ci, d)[0], RF.at[pl.ds(3 * e, 1), from_x(d)], ls.at[d])

    def right_start(ci, d):
        right_pair(ci, d).start()

        @pl.when(own[ci])
        def _():
            right_here(ci, d).start()

        @pl.when(jnp.logical_not(own[ci]))
        def _():
            right_single(ci, d).start()

    def right_sent(ci, d):
        right_pair(ci, d).wait_send()

        @pl.when(own[ci])
        def _():
            right_here(ci, d).wait()

        @pl.when(jnp.logical_not(own[ci]))
        def _():
            right_single(ci, d).wait_send()

    def single_arrived(at):
        @pl.when(jnp.logical_not(jnp.logical_and(any_own, at // 4 == yh)))
        def _():
            remote(F.at[pl.ds(0, 1)], RF.at[pl.ds(3 * e, 1), at], ss.at[0, 0], rs.at[at], across).wait_recv()

    def pair_arrived(at):
        remote(F.at[pl.ds(0, 2)], RF.at[pl.ds(1, 2), at], sp.at[0, 0], rp.at[at], across).wait_recv()

    def hand(at):
        return remote(RF.at[pl.ds(1 + e, 1), at], RF.at[pl.ds(3 * e, 1), at], sf.at[at], rf.at[at], sibling)

    def handed(at):
        remote(F.at[pl.ds(0, 1)], RF.at[pl.ds(3 - 3 * e, 1), at], sf.at[at], rf.at[at], sibling).wait_recv()

    here = [
        pltpu.make_async_copy(F.at[pl.ds((row + 2 * col + t) % 16, 1)], LF.at[col, pl.ds(t, 1)], ls.at[4 + t])
        for t in range(3)
    ]
    here_across = pltpu.make_async_copy(LY.at[pl.ds(2 * x, 3)], LF.at[other + x], ls.at[7])

    order = (2, 1, 3)
    for d in order:
        for ci in range(2):
            spread(d, ci).start()
    for t in range(9):
        cross(t).start()
    for ci in range(2):
        right_start(ci, 0)
    for d in order:
        for t in range(3):
            left_own(d, t, col).start()
    for copy in here:
        copy.start()
    for d in order:
        for ci in range(2):
            spread(d, ci).wait_recv()
            right_start(ci, d)
    for t in range(9):
        cross(t).wait_recv()
    here_across.start()
    for d in order:
        left_across(d, other + x).start()
    for at in range(8):
        pair_arrived(at)
        hand(at).start()
    for d in order:
        for t in range(3):
            left_own(d, t, from_x(d)).wait_recv()
        left_across(d, other + (x + 4 - d) % 4).wait_recv()
    for at in range(8):
        single_arrived(at)
    for at in range(8):
        handed(at)
    for copy in here:
        copy.wait()
    here_across.wait()
    for d in order:
        for ci in range(2):
            spread(d, ci).wait_send()
        for t in range(3):
            left_own(d, t, col).wait_send()
        left_across(d, other + x).wait_send()
    for t in range(9):
        cross(t).wait_send()
    for ci in range(2):
        for d in range(4):
            right_sent(ci, d)
    for at in range(8):
        hand(at).wait_send()


def exchange(f):
    unit = (ROWS, LANES)
    sems = ((3, 2), (9,), (3, 3), (3,))
    return pl.pallas_call(
        exchange_kernel,
        out_shape=[jax.ShapeDtypeStruct((4, 8) + unit, BF16), jax.ShapeDtypeStruct((8, 3) + unit, BF16)],
        in_specs=[pl.BlockSpec(memory_space=pl.ANY)],
        out_specs=[pl.BlockSpec(memory_space=pl.ANY)] * 2,
        scratch_shapes=[pltpu.VMEM((2, 3, 2) + unit, BF16), pltpu.VMEM((9,) + unit, BF16)]
        + [DMA(shape) for shape in sems for _ in range(2)]
        + [DMA((2, 4)), DMA((8,)), DMA((2, 4)), DMA((8,)), DMA((8,)), DMA((8,)), DMA((8,))],
        compiler_params=pltpu.CompilerParams(
            collective_id=0, has_side_effects=True, vmem_limit_bytes=32 << 20
        ),
        name="exchange",
    )(f)


def window(parts, r):
    a, o = divmod(BLK * r, 128)
    if o + BLK <= 128:
        return parts[a], o
    return jnp.where(lane_ids(Q) >= o, parts[a], parts[a + 1]), o


def product_kernel(rf, lf, out, left, first, middle, last, total, lscr, colv, cols, csem, osem):
    lane8 = lane_ids(Q)
    for n in range(56):
        row = rf[n // 8, n % 8, 0:16, 512:640] if n < 32 else lf[(n - 32) // 3, (n - 32) % 3, 0:16, 512:640]
        colv[n : n + 1, :] = row.astype(F32)[0:1].astype(jnp.int32)
    ccopy = pltpu.make_async_copy(colv, cols, csem)
    ccopy.start()

    def clear(k, _):
        first[k] = jnp.zeros(first.shape[1:], BF16)
        middle[k] = jnp.zeros(middle.shape[1:], BF16)
        last[k] = jnp.zeros(last.shape[1:], BF16)
        return 0

    lax.fori_loop(0, BB, clear, 0)
    lscr[...] = jnp.zeros_like(lscr)
    for i8 in range(8):
        shift = (BLK * i8) % 8

        def left_rows(n, _):
            h = n // 3
            s = n - 3 * h
            cs = 4 * h + i8 // 2
            x = lf[cs, s].astype(F32)
            blocks = []
            for p in range(PG):
                at = ((i8 % 2) * PG + p) * Q
                blocks.append([x[at : at + Q, 128 * t : 128 * (t + 1)] for t in range(5)])
            for r in range(RR):
                rolled = []
                for p in range(PG):
                    v, o = window(blocks[p], r)
                    amount = (KP * p - o) % 128
                    rolled.append(pltpu.roll(v, amount, 1) if amount else v)
                t0 = jnp.where(lane8 < BLK, rolled[0], jnp.where(lane8 >= KP, rolled[1], 0.0))
                e1 = KP + BLK - 128
                s2 = 2 * KP - 128
                t1 = jnp.where(
                    lane8 < e1,
                    rolled[1],
                    jnp.where(jnp.logical_and(lane8 >= s2, lane8 < s2 + BLK), rolled[2], 0.0),
                )
                lscr[0, pl.ds(shift + r, Q, stride=RR), :] = t0
                lscr[1, pl.ds(shift + r, Q, stride=RR), :] = t1
            left[s, 8 * h + i8, :, 0:128] = lscr[0].astype(BF16)
            left[s, 8 * h + i8, :, 128:256] = lscr[1].astype(BF16)
            return 0

        if shift:
            lscr[:, 0:8, :] = jnp.zeros((2, 8, 128), F32)
        lscr[:, 72:80, :] = jnp.zeros((2, 8, 128), F32)
        lax.fori_loop(0, 6, left_rows, 0)
    source = lax.broadcasted_iota(jnp.int32, (256, 256), 0)
    target = lax.broadcasted_iota(jnp.int32, (256, 256), 1)
    block = source // KP
    c = source - KP * block
    moved = KP * block + Q * (c % RR) + c // RR
    order = jnp.logical_and(target == moved, c < BLK).astype(F32).astype(BF16)

    def reorder(n, _):
        s = n // 4
        at = pl.ds((n - 4 * s) * 4, 4)
        rows = left[s, at].reshape(4 * KP, 256)
        rows = jnp.dot(rows, order, preferred_element_type=F32).astype(BF16)
        left[s, at] = rows.reshape(4, KP, 256)
        return 0

    lax.fori_loop(0, 12, reorder, 0)
    ccopy.wait()

    for slot, (dest, base) in enumerate(((first, 0), (middle, 0), (middle, 16 * BLK), (last, 16 * BLK - 1024))):
        top = dest.shape[2] // 128 - 1

        def expand(cs, _, slot=slot, dest=dest, base=base, top=top):
            x = rf[slot, cs].astype(F32)
            for k2 in range(2):
                for p in range(PG):
                    at = (k2 * PG + p) * Q
                    parts = [x[at : at + Q, 128 * t : 128 * (t + 1)] for t in range(5)]
                    j = cols[slot * 8 + cs, CHUNK - 512 + k2 * PG + p]
                    start = base + BLK * j
                    t = start // 128
                    d = start - 128 * t
                    mask_low = jnp.logical_and(lane8 >= d, lane8 < d + BLK)
                    mask_high = lane8 < d + BLK - 128
                    lows, highs = [], []
                    for r in range(RR):
                        v, o = window(parts, r)
                        v = pltpu.roll(v, (d + 128 - o) % 128, 1)
                        lows.append(jnp.where(mask_low, v, 0.0))
                        highs.append(jnp.where(mask_high, v, 0.0))
                    zero = jnp.zeros((Q, 128), F32)
                    low = jnp.concatenate(lows + [zero], axis=0).astype(BF16)
                    high = jnp.concatenate(highs + [zero], axis=0).astype(BF16)
                    k = 2 * cs + k2
                    tl = pl.ds(pl.multiple_of(t * 128, 128), 128)
                    th = pl.ds(pl.multiple_of(jnp.minimum(t + 1, top) * 128, 128), 128)
                    dest[k, :, tl] += low
                    dest[k, :, th] += high
            return 0

        lax.fori_loop(0, 8, expand, 0)

    total[0:8, :] = jnp.zeros((8, total.shape[1]), F32)

    def copy_out(i, rows):
        at = pl.ds(pl.multiple_of(64 * i, 8), rows)
        return pltpu.make_async_copy(total.at[at], out.at[at], osem.at[i])

    def multiply(i, _):
        ks = [
            [cols[32 + (i // 2) * 3 + s, CHUNK - 512 + (i % 2) * PG + p] for p in range(PG)]
            for s in range(3)
        ]
        ls = [left[s, i][:, : PG * KP] for s in range(3)]
        base = pl.multiple_of((BLK * i // 8) * 8, 8)
        for n in range(9):
            lanes = slice(256 * n, 256 * (n + 1))
            acc = jnp.dot(
                ls[1],
                jnp.concatenate([middle[k, :, lanes] for k in ks[1]], axis=0),
                preferred_element_type=F32,
            )
            if n < 5:
                acc += jnp.dot(
                    ls[0],
                    jnp.concatenate([first[k, :, lanes] for k in ks[0]], axis=0),
                    preferred_element_type=F32,
                )
            if n >= 4:
                lanes = slice(256 * (n - 4), 256 * (n - 3))
                acc += jnp.dot(
                    ls[2],
                    jnp.concatenate([last[k, :, lanes] for k in ks[2]], axis=0),
                    preferred_element_type=F32,
                )
            width = min(256, total.shape[1] - 256 * n)
            lanes = slice(256 * n, 256 * n + width)
            total[pl.ds(base, 8), lanes] += acc[0:8, :width]
            total[pl.ds(base + 8, 72), lanes] = acc[8:80, :width]
        copy_out(i, 64).start()
        return 0

    lax.fori_loop(0, BB, multiply, 0)
    copy_out(16, 80).start()
    for i in range(16):
        copy_out(i, 64).wait()
    copy_out(16, 80).wait()


def product(rf, lf):
    return pl.pallas_call(
        product_kernel,
        out_shape=jax.ShapeDtypeStruct((BB * BLK, 2 * BB * BLK), F32),
        in_specs=[pl.BlockSpec(memory_space=pltpu.VMEM)] * 2,
        out_specs=pl.BlockSpec(memory_space=pl.ANY),
        scratch_shapes=[
            pltpu.VMEM((3, BB, KP, 256), BF16),
            pltpu.VMEM((BB, KP, 1280), BF16),
            pltpu.VMEM((BB, KP, 2304), BF16),
            pltpu.VMEM((BB, KP, 1280), BF16),
            pltpu.VMEM((BB * BLK + 8, 2 * BB * BLK), F32),
            pltpu.VMEM((2, KP, 128), F32),
            pltpu.VMEM((56, 128), jnp.int32),
            pltpu.SMEM((56, 128), jnp.int32),
            DMA,
            DMA((17,)),
        ],
        compiler_params=pltpu.CompilerParams(vmem_limit_bytes=48 << 20),
        name="product",
    )(rf, lf)


def shards(x_blocks, x_cols):
    rf, lf = exchange(pack(x_blocks, x_cols))
    return product(rf, lf)


def solution(mesh):
    in_specs = (P(("row", "col"), None, None, None), P(("row", "col"), None, None))
    return jax.shard_map(shards, mesh=mesh, in_specs=in_specs, out_specs=P("row", "col"), check_vma=False)
```

```python
import jax
import jax.numpy as jnp
from jax import lax
from jax.experimental import pallas as pl
from jax.experimental.pallas import tpu as pltpu
from jax.sharding import PartitionSpec as P

BLK = 69
BB = 16
PG = 3
GROUPS = 16
Q = 8
RR = 9
CHUNK = RR * BLK
ROWS = 2 * PG * Q
LANES = 640
TAIL = CHUNK - 512
KP = 80
WIDE = 1280
SIZE = BLK * BLK
F32 = jnp.float32
BF16 = jnp.bfloat16
MESH = pl.DeviceIdType.MESH
DMA = pltpu.SemaphoreType.DMA


def lane_ids(rows):
    return lax.broadcasted_iota(jnp.int32, (rows, 128), 1)


def pack(cols_ref, x_ref, f_ref, scr):
    tiles = (SIZE + 127) // 128
    lane = lane_ids(Q)

    def some(n, _):
        for h in range(2):
            flat = x_ref[n, Q * h : Q * h + Q].astype(F32)
            parts = [flat[:, 128 * t : 128 * (t + 1)] for t in range(tiles - 1)]
            rest = jnp.zeros((Q, 128 * tiles - SIZE), F32)
            parts.append(jnp.concatenate([flat[:, 128 * (tiles - 1) : SIZE], rest], axis=1))
            parts.append(jnp.zeros((Q, 128), F32))
            for q in range(Q):
                for t in range(LANES // 128):
                    a, o = divmod(CHUNK * q + 128 * t, 128)
                    if a >= tiles:
                        piece = parts[tiles]
                    elif o:
                        piece = pltpu.roll(jnp.where(lane >= o, parts[a], parts[a + 1]), 128 - o, 1)
                    else:
                        piece = parts[a]
                    scr[t, pl.ds(Q * h * ROWS + n * Q + q, Q, stride=ROWS), :] = piece
        return 0

    lax.fori_loop(0, 2 * PG, some, 0)
    lane_all = lane_ids(ROWS)

    def group(g, _):
        at = pl.ds(pl.multiple_of(g * ROWS, 16), ROWS)
        for t in range(4):
            f_ref[g, :, 128 * t : 128 * (t + 1)] = scr[t, at, :].astype(BF16)
        tail = jnp.where(lane_all < TAIL, scr[4, at, :], 0.0)
        for k2 in range(2):
            for p in range(PG):
                value = cols_ref[k2, p, g].astype(F32)
                tail = jnp.where(lane_all == TAIL + k2 * PG + p, value, tail)
        f_ref[g, :, 512:640] = tail.astype(BF16)
        return 0

    lax.fori_loop(0, GROUPS, group, 0)


LEFT_AT = [min(BLK * r // 128, 3) for r in range(RR)]
RIGHT_AT = [min(2 * BLK * u // 128, 3) for u in range((RR + 1) // 2)]


def build_left_windows(ref):
    source = lax.broadcasted_iota(jnp.int32, (256, 256), 0)
    target = lax.broadcasted_iota(jnp.int32, (256, 256), 1)
    place = target - KP * (target // KP)
    q = place - Q * (place // Q)
    wanted = jnp.where(target < PG * KP, RR * q + place // Q, BLK)
    wanted = jnp.where(place < Q * RR, wanted, BLK)
    gap = jnp.where(wanted < BLK, source - wanted, -1024)

    def one(r, _):
        start = BLK * r - 128 * jnp.minimum(BLK * r // 128, 3)
        ref[r] = jnp.where(gap == start, 1.0, 0.0).astype(BF16)
        return 0

    lax.fori_loop(0, RR, one, 0)


def build_right_windows(ref):
    source = lax.broadcasted_iota(jnp.int32, (256, 256), 0)
    target = lax.broadcasted_iota(jnp.int32, (256, 256), 1)
    half = target // 128
    b = target - 128 * half
    gap = jnp.where(b < BLK, source - b - BLK * half, -1024)

    def one(u, _):
        start = 2 * BLK * u - 128 * jnp.minimum(2 * BLK * u // 128, 3)
        keep = jnp.logical_or(half == 0, u < RR // 2)
        ref[u] = jnp.where(jnp.logical_and(gap == start, keep), 1.0, 0.0).astype(BF16)
        return 0

    lax.fori_loop(0, (RR + 1) // 2, one, 0)


def window(x, ref, n, at):
    return jnp.dot(x[:, 128 * at : 128 * at + 256], ref[n], preferred_element_type=F32)


def unpack_left(x, windows, scr, left, cs):
    lane = lane_ids(Q)
    first = 2 * cs
    shifts = [(5 * (first + k2)) % 8 for k2 in range(2)]
    for n in range(2 * PG):
        for t in range(2):
            scr[n, t, 0:8, :] = jnp.zeros((8, 128), F32)
            scr[n, t, 72:80, :] = jnp.zeros((8, 128), F32)
    for r in range(RR):
        y = window(x, windows, r, LEFT_AT[r])
        for n in range(2 * PG):
            at = n * PG * Q
            e0, e1, e2 = (y[at + Q * p : at + Q * (p + 1)] for p in range(PG))
            low = jnp.where(lane < KP, e0[:, :128], e1[:, :128])
            high = jnp.where(lane < 2 * KP - 128, e1[:, 128:], e2[:, 128:])
            rows = pl.ds(shifts[n % 2] + r, Q, stride=RR)
            scr[n, 0, rows, :] = low
            scr[n, 1, rows, :] = high
    for n in range(2 * PG):
        for t in range(2):
            left[n // 2, first + n % 2, :, 128 * t : 128 * (t + 1)] = scr[n, t].astype(BF16)


def unpack_right(x, windows, compact, slots, cs):
    for u in range((RR + 1) // 2):
        y = window(x, windows, u, RIGHT_AT[u])
        for n, slot in enumerate(slots):
            for k2 in range(2):
                for p in range(PG):
                    at = n * ROWS + (k2 * PG + p) * Q
                    both = jnp.concatenate([y[at : at + Q, :128], y[at : at + Q, 128:]], axis=0)
                    compact[slot, 2 * cs + k2, p, 16 * u : 16 * u + 16, :] = both.astype(BF16)


def put_columns(colv, n, row):
    colv[pl.ds(n, 1), :] = row.astype(F32)[0:1].astype(jnp.int32)

def exchange_kernel(
    xc, xb, colv, left, compact, F, fscr, RX, LY, ZS, ZP, RF, LF, lscr, winl, winr,
    sa, ra, sb, rb, so, ro, sl, rl, s1, r1, s2, rs, rp, sf, rf, ls,
):
    row = lax.axis_index("row")
    col = lax.axis_index("col")
    z, yl, m, e = row // 4, (row // 2) % 2, row // 2, row % 2
    yh, x = col // 4, col % 4
    no, both, either = jnp.logical_not, jnp.logical_and, jnp.logical_or

    def remote(src, dst, send, recv, device):
        return pltpu.make_async_remote_copy(
            src_ref=src, dst_ref=dst, send_sem=send, recv_sem=recv, device_id=device, device_id_type=MESH
        )

    at_x = [(x + d) % 4 for d in range(4)]
    peers = {d: (row, yh * 4 + at_x[d]) for d in (1, 2, 3)}
    across = (row, (1 - yh) * 4 + x)
    sibling = (row + 1 - 2 * e, col)

    plan = {}
    for ci in range(2):
        C = x + 4 * ci
        for kind in range(2):
            b = e if kind == 0 else 1 - e
            u = yl - C - b + 16
            yl2, dz = u % 2, (u // 2) % 4
            stay_z = dz == 0
            stay_y = both(yh == ci, yl2 == yl)
            to_z = (z + dz) % 4
            plan[ci, kind] = dict(
                relay=both(no(stay_z), no(stay_y)),
                hop=(to_z * 4 + yl * 2 + e, col),
                hop_from=(((z - dz + 4) % 4) * 4 + yl * 2 + e, col),
                final=(jnp.where(stay_y, to_z, z) * 4 + yl2 * 2 + b, C),
                here=both(both(stay_z, stay_y), b == e),
            )
    senders = []
    ms = m + col + e
    for kind in range(2):
        es = e if kind == 0 else 1 - e
        for h in range(2):
            zs = jnp.where(both(yh == h, ms % 2 == yl), (ms // 2) % 4, z)
            device = (zs * 4 + (ms % 2) * 2 + es, h * 4 + x)
            senders.append((device, both(device[0] == row, device[1] == col)))

    barrier = pltpu.get_barrier_semaphore()

    def greet(device):
        pl.semaphore_signal(barrier, 1, device_id=device, device_id_type=MESH)

    for device in (peers[1], peers[2], peers[3], across, sibling):
        greet(device)
    count = jnp.int32(5)
    for v in plan.values():

        @pl.when(v["relay"])
        def _(v=v):
            greet(v["hop"])
            greet(v["hop_from"])

        @pl.when(no(v["here"]))
        def _(v=v):
            greet(v["final"])

        count = count + jnp.where(v["relay"], 2, 0) + jnp.where(v["here"], 0, 1)
    for device, mine in senders:

        @pl.when(no(mine))
        def _(device=device):
            greet(device)

        count = count + jnp.where(mine, 0, 1)

    pack(xc, xb, F, fscr)
    pl.semaphore_wait(barrier, count)

    def one(ref, i):
        return ref.at[pl.ds(i, 1)]

    def groups_at(place, ci):
        return 2 * place + 8 * ci

    def spread(d, ci):
        src = F.at[pl.ds(groups_at(at_x[d], ci), 2)]
        return remote(src, RX.at[ci, d - 1], sa.at[d - 1, ci], ra.at[d - 1, ci], peers[d])

    def cross(t):
        return remote(one(F, (row + 8 * (1 - yh) + t) % 16), one(LY, t), sb.at[t], rb.at[t], across)

    def left_own(d, t, at):
        src = one(F, (row + 2 * (yh * 4 + at_x[d]) + t) % 16)
        return remote(src, LF.at[at, pl.ds(t, 1)], so.at[d - 1, t], ro.at[d - 1, t], peers[d])

    other = (1 - yh) * 4

    def left_across(d, at):
        return remote(LY.at[pl.ds(2 * at_x[d], 3)], LF.at[at], sl.at[d - 1], rl.at[d - 1], peers[d])

    def from_x(d):
        return yh * 4 + (x + 4 - d) % 4

    def right_src(ci, kind, d):
        if d == 0:
            return one(F, groups_at(x, ci) + e) if kind == 0 else F.at[pl.ds(groups_at(x, ci), 2)]
        return RX.at[ci, d - 1, pl.ds(e, 1)] if kind == 0 else RX.at[ci, d - 1]

    def right_dst(kind, d):
        return RF.at[pl.ds(3 * e, 1), from_x(d)] if kind == 0 else RF.at[pl.ds(1, 2), from_x(d)]

    def relay_at(ci, kind, d):
        return ZS.at[ci, d] if kind == 0 else ZP.at[ci, d]

    def arrive(kind, at):
        return rs.at[at] if kind == 0 else rp.at[at]

    def direct(ci, kind, d):
        to = plan[ci, kind]["final"]
        return remote(right_src(ci, kind, d), right_dst(kind, d), s1.at[ci, kind, d], arrive(kind, from_x(d)), to)

    def hop(ci, kind, d):
        to = plan[ci, kind]["hop"]
        return remote(right_src(ci, kind, d), relay_at(ci, kind, d), s1.at[ci, kind, d], r1.at[ci, kind, d], to)

    def last(ci, kind, d):
        to = plan[ci, kind]["final"]
        return remote(relay_at(ci, kind, d), right_dst(kind, d), s2.at[ci, kind, d], arrive(kind, from_x(d)), to)

    def stay(ci, d):
        return pltpu.make_async_copy(right_src(ci, 0, d), right_dst(0, d), ls.at[d])

    def right_start(ci, d):
        for kind in (1, 0):
            v = plan[ci, kind]

            @pl.when(v["relay"])
            def _():
                hop(ci, kind, d).start()

            if kind == 0:

                @pl.when(v["here"])
                def _():
                    stay(ci, d).start()

            @pl.when(no(either(v["relay"], v["here"])))
            def _():
                direct(ci, kind, d).start()

    def right_relay(ci, d):
        for kind in (1, 0):

            @pl.when(plan[ci, kind]["relay"])
            def _():
                hop(ci, kind, d).wait_recv()
                last(ci, kind, d).start()

    def right_sent(ci, d):
        for kind in (1, 0):
            v = plan[ci, kind]

            @pl.when(v["relay"])
            def _():
                hop(ci, kind, d).wait_send()
                last(ci, kind, d).wait_send()

            @pl.when(no(either(v["relay"], v["here"])))
            def _():
                direct(ci, kind, d).wait_send()

    any_here = either(plan[0, 0]["here"], plan[1, 0]["here"])

    def single_arrived(at):
        mine = both(any_here, at // 4 == yh)

        @pl.when(no(mine))
        def _():
            remote(F.at[pl.ds(0, 1)], RF.at[pl.ds(3 * e, 1), at], s1.at[0, 0, 0], rs.at[at], across).wait_recv()

        @pl.when(mine)
        def _():
            d = (x + 4 - at % 4) % 4
            pltpu.make_async_copy(F.at[pl.ds(0, 1)], RF.at[pl.ds(3 * e, 1), at], ls.at[d]).wait()

    def pair_arrived(at):
        remote(F.at[pl.ds(0, 2)], RF.at[pl.ds(1, 2), at], s1.at[0, 0, 0], rp.at[at], across).wait_recv()

    def hand(at):
        return remote(RF.at[pl.ds(1 + e, 1), at], RF.at[pl.ds(3 * e, 1), at], sf.at[at], rf.at[at], sibling)

    def handed(at):
        remote(F.at[pl.ds(0, 1)], RF.at[pl.ds(3 - 3 * e, 1), at], sf.at[at], rf.at[at], sibling).wait_recv()

    def take_left(packets, cs):
        for t in range(PG):
            put_columns(colv, 32 + cs * 3 + t, packets(t)[0:16, 512:640])
        rows = jnp.concatenate([packets(t) for t in range(PG)], axis=0)
        unpack_left(rows, winl, lscr, left, cs)

    def take_left_at(cs):
        take_left(lambda t: LF[cs, t], cs)

    def take_right(slots, cs):
        for slot in slots:
            put_columns(colv, slot * 8 + cs, RF[slot, cs, 0:16, 512:640])
        rows = jnp.concatenate([RF[slot, cs] for slot in slots], axis=0)
        unpack_right(rows, winr, compact, slots, cs)

    order = (2, 1, 3)
    for d in order:
        for ci in range(2):
            spread(d, ci).start()
    for t in range(9):
        cross(t).start()
    for ci in range(2):
        right_start(ci, 0)
    build_left_windows(winl)
    build_right_windows(winr)
    for n, d in enumerate(order):
        for ci in range(2):
            spread(d, ci).wait_recv()
            right_start(ci, d)
        for t in range(3):
            left_own(d, t, col).start()
        for ci in range(2):
            right_relay(ci, 0 if n == 0 else order[n - 1])
    for t in range(9):
        cross(t).wait_recv()
    for d in order:
        left_across(d, other + x).start()
    for ci in range(2):
        right_relay(ci, order[2])
    take_left(lambda t: F[(row + 2 * col + t) % 16], col)
    take_left(lambda t: LY[2 * x + t], other + x)

    def place(n):
        d = n // 2
        d = jnp.where(d == 0, 0, jnp.where(d == 1, order[0], jnp.where(d == 2, order[1], order[2])))
        h = jnp.where(n % 2 == 0, yh, 1 - yh)
        return h * 4 + (x + 4 - d) % 4

    def pairs(n, _):
        at = place(n)
        pair_arrived(at)
        hand(at).start()
        take_right((1, 2), at)
        return 0

    lax.fori_loop(0, 8, pairs, 0)
    for d in order:
        for t in range(3):
            left_own(d, t, from_x(d)).wait_recv()
        take_left_at(from_x(d))

    def singles(n, _):
        at = place(n)
        single_arrived(at)
        handed(at)
        take_right((0, 3), at)
        return 0

    lax.fori_loop(0, 8, singles, 0)
    for d in order:
        at = other + (x + 4 - d) % 4
        left_across(d, at).wait_recv()
        take_left_at(at)
    for d in order:
        for ci in range(2):
            spread(d, ci).wait_send()
        for t in range(3):
            left_own(d, t, col).wait_send()
        left_across(d, other + x).wait_send()
    for t in range(9):
        cross(t).wait_send()
    for ci in range(2):
        for d in range(4):
            right_sent(ci, d)
    for at in range(8):
        hand(at).wait_send()


def exchange(x_cols, x_blocks):
    unit = (ROWS, LANES)
    return pl.pallas_call(
        exchange_kernel,
        out_shape=[
            jax.ShapeDtypeStruct((56, 128), jnp.int32),
            jax.ShapeDtypeStruct((3, BB, KP, 256), BF16),
            jax.ShapeDtypeStruct((4, BB, PG, KP, 128), BF16),
        ],
        in_specs=[pl.BlockSpec(memory_space=pltpu.SMEM), pl.BlockSpec(memory_space=pltpu.VMEM)],
        out_specs=[pl.BlockSpec(memory_space=pltpu.VMEM)] * 3,
        scratch_shapes=[
            pltpu.VMEM((GROUPS,) + unit, BF16),
            pltpu.VMEM((LANES // 128, GROUPS * ROWS, 128), F32),
            pltpu.VMEM((2, 3, 2) + unit, BF16),
            pltpu.VMEM((9,) + unit, BF16),
            pltpu.VMEM((2, 4, 1) + unit, BF16),
            pltpu.VMEM((2, 4, 2) + unit, BF16),
            pltpu.VMEM((4, 8) + unit, BF16),
            pltpu.VMEM((8, 3) + unit, BF16),
            pltpu.VMEM((2 * PG, 2, KP, 128), F32),
            pltpu.VMEM((RR, 256, 256), BF16),
            pltpu.VMEM(((RR + 1) // 2, 256, 256), BF16),
        ]
        + [DMA(shape) for shape in ((3, 2), (9,), (3, 3), (3,), (2, 2, 4)) for _ in range(2)]
        + [DMA((2, 2, 4))]
        + [DMA((8,)) for _ in range(5)],
        compiler_params=pltpu.CompilerParams(
            collective_id=0, has_side_effects=True, vmem_limit_bytes=40 << 20
        ),
        name="exchange",
    )(x_cols, x_blocks)


def expand(compact, dense, cols, slot, at, k):
    lane = lane_ids(KP)
    shift = 16 * BLK - 1024 if slot >= 2 else 0
    dense[at, k] = jnp.zeros((KP, WIDE), BF16)
    for p in range(PG):
        start = shift + BLK * cols[slot * 8 + k // 2, TAIL + (k % 2) * PG + p]
        t = start // 128
        d = start - 128 * t
        y = pltpu.roll(compact[slot, k, p], d, 1)
        zero = jnp.zeros_like(y)
        low = pl.ds(pl.multiple_of(128 * t, 128), 128)
        high = pl.ds(pl.multiple_of(128 * t + 128, 128), 128)
        dense[at, k, :, low] += jnp.where(lane >= d, y, zero)
        dense[at, k, :, high] += jnp.where(lane < d, y, zero)


def product_kernel(cols, left, compact, out, even, odd, total, osem):
    def rows_of(i, j, rows):
        at = pl.ds(pl.multiple_of(64 * i, 8), rows)
        lanes = pl.ds(0, 1024) if j == 0 else pl.ds(1024, 2 * BB * BLK - 1024)
        return pltpu.make_async_copy(total.at[at, lanes], out.at[at, lanes], osem.at[j, i])

    def first(n, _):
        for k in (2 * n, 2 * n + 1):
            for slot in range(2):
                expand(compact, even, cols, slot, slot, k)
        return 0

    lax.fori_loop(0, BB // 2, first, 0)
    total[0:8, :] = jnp.zeros((8, total.shape[1]), F32)

    def multiply(i, j, dense):
        ls = [left[j + s, i][:, : PG * KP] for s in range(2)]
        ks = [
            [cols[32 + (i // 2) * 3 + j + s, TAIL + (i % 2) * PG + p] for p in range(PG)] for s in range(2)
        ]
        base = pl.multiple_of((BLK * i // 8) * 8, 8)
        for n in range(5):
            acc = None
            for s in range(2):
                w = jnp.concatenate([dense[s, k, :, 256 * n : 256 * (n + 1)] for k in ks[s]], axis=0)
                term = jnp.dot(ls[s], w, preferred_element_type=F32)
                acc = term if acc is None else acc + term
            lo = 1024 * j + 256 * n
            width = min(256, total.shape[1] - lo)
            lanes = slice(lo, lo + width)
            if j == 1 and n == 0:
                total[pl.ds(base, 80), lanes] += acc
            else:
                total[pl.ds(base, 8), lanes] += acc[0:8, :width]
                total[pl.ds(base + 8, 72), lanes] = acc[8:80, :width]

    def second(i, _):
        multiply(i, 0, even)
        for slot in range(2, 4):
            expand(compact, odd, cols, slot, slot - 2, i)
        rows_of(i, 0, 64).start()
        return 0

    lax.fori_loop(0, BB, second, 0)
    rows_of(16, 0, 80).start()

    def third(i, _):
        multiply(i, 1, odd)
        rows_of(i, 1, 64).start()
        return 0

    lax.fori_loop(0, BB, third, 0)
    rows_of(16, 1, 80).start()
    for j in range(2):
        for i in range(16):
            rows_of(i, j, 64).wait()
        rows_of(16, j, 80).wait()


def product(cols, left, compact):
    return pl.pallas_call(
        product_kernel,
        out_shape=jax.ShapeDtypeStruct((BB * BLK, 2 * BB * BLK), F32),
        in_specs=[pl.BlockSpec(memory_space=pltpu.SMEM)] + [pl.BlockSpec(memory_space=pltpu.VMEM)] * 2,
        out_specs=pl.BlockSpec(memory_space=pl.ANY),
        scratch_shapes=[
            pltpu.VMEM((2, BB, KP, WIDE), BF16),
            pltpu.VMEM((2, BB, KP, WIDE), BF16),
            pltpu.VMEM((BB * BLK + 8, 2 * BB * BLK), F32),
            DMA((2, 17)),
        ],
        compiler_params=pltpu.CompilerParams(vmem_limit_bytes=36 << 20),
        name="product",
    )(cols, left, compact)


def shards(x_blocks, x_cols):
    cols, left, compact = exchange(
        x_cols.transpose(0, 2, 1), x_blocks.transpose(0, 2, 1, 3).reshape(2 * PG, GROUPS, SIZE)
    )
    return product(cols, left, compact)


def solution(mesh):
    in_specs = (P(("row", "col"), None, None, None), P(("row", "col"), None, None))
    return jax.shard_map(shards, mesh=mesh, in_specs=in_specs, out_specs=P("row", "col"), check_vma=False)
```

```python
import jax
import jax.numpy as jnp
from jax import lax
from jax.experimental import pallas as pl
from jax.experimental.pallas import tpu as pltpu
from jax.sharding import PartitionSpec as P

BLK = 69
BB = 16
PG = 3
GROUPS = 16
Q = 8
RR = 9
CHUNK = RR * BLK
ROWS = 2 * PG * Q
LANES = 640
TAIL = CHUNK - 512
KP = 80
WIDE = 1280
KEPT = 25
SIZE = BLK * BLK
F32 = jnp.float32
BF16 = jnp.bfloat16
MESH = pl.DeviceIdType.MESH
DMA = pltpu.SemaphoreType.DMA


def lane_ids(rows):
    return lax.broadcasted_iota(jnp.int32, (rows, 128), 1)


def pack(cols_ref, x_ref, f_ref, scr):
    tiles = (SIZE + 127) // 128
    lane = lane_ids(Q)

    def some(n, _):
        for h in range(2):
            flat = x_ref[n, Q * h : Q * h + Q].astype(F32)
            parts = [flat[:, 128 * t : 128 * (t + 1)] for t in range(tiles - 1)]
            rest = jnp.zeros((Q, 128 * tiles - SIZE), F32)
            parts.append(jnp.concatenate([flat[:, 128 * (tiles - 1) : SIZE], rest], axis=1))
            parts.append(jnp.zeros((Q, 128), F32))
            for q in range(Q):
                for t in range(LANES // 128):
                    a, o = divmod(CHUNK * q + 128 * t, 128)
                    if a >= tiles:
                        piece = parts[tiles]
                    elif o:
                        piece = pltpu.roll(jnp.where(lane >= o, parts[a], parts[a + 1]), 128 - o, 1)
                    else:
                        piece = parts[a]
                    scr[t, pl.ds(Q * h * ROWS + n * Q + q, Q, stride=ROWS), :] = piece
        return 0

    lax.fori_loop(0, 2 * PG, some, 0)
    lane_all = lane_ids(ROWS)

    def group(g, _):
        at = pl.ds(pl.multiple_of(g * ROWS, 16), ROWS)
        for t in range(4):
            f_ref[g, :, 128 * t : 128 * (t + 1)] = scr[t, at, :].astype(BF16)
        tail = jnp.where(lane_all < TAIL, scr[4, at, :], 0.0)
        for k2 in range(2):
            for p in range(PG):
                value = cols_ref[p, k2, g].astype(F32)
                tail = jnp.where(lane_all == TAIL + k2 * PG + p, value, tail)
        f_ref[g, :, 512:640] = tail.astype(BF16)

        @pl.when(g < KEPT - GROUPS)
        def _():
            f_ref[g + GROUPS] = f_ref[g]

        return 0

    lax.fori_loop(0, GROUPS, group, 0)


LEFT_AT = [min(BLK * r // 128, 3) for r in range(RR)]
RIGHT_AT = [min(2 * BLK * u // 128, 3) for u in range((RR + 1) // 2)]


def build_left_windows(ref):
    source = lax.broadcasted_iota(jnp.int32, (256, 256), 0)
    target = lax.broadcasted_iota(jnp.int32, (256, 256), 1)
    place = target - KP * (target // KP)
    q = place - Q * (place // Q)
    wanted = jnp.where(target < PG * KP, RR * q + place // Q, BLK)
    wanted = jnp.where(place < Q * RR, wanted, BLK)
    gap = jnp.where(wanted < BLK, source - wanted, -1024)

    def one(r, _):
        start = BLK * r - 128 * jnp.minimum(BLK * r // 128, 3)
        ref[r] = jnp.where(gap == start, 1.0, 0.0).astype(BF16)
        return 0

    lax.fori_loop(0, RR, one, 0)


def build_right_windows(ref):
    source = lax.broadcasted_iota(jnp.int32, (256, 256), 0)
    target = lax.broadcasted_iota(jnp.int32, (256, 256), 1)
    half = target // 128
    b = target - 128 * half
    gap = jnp.where(b < BLK, source - b - BLK * half, -1024)

    def one(u, _):
        start = 2 * BLK * u - 128 * jnp.minimum(2 * BLK * u // 128, 3)
        keep = jnp.logical_or(half == 0, u < RR // 2)
        ref[u] = jnp.where(jnp.logical_and(gap == start, keep), 1.0, 0.0).astype(BF16)
        return 0

    lax.fori_loop(0, (RR + 1) // 2, one, 0)


def window(x, ref, n, at):
    return jnp.dot(x[:, 128 * at : 128 * at + 256], ref[n], preferred_element_type=F32)


def unpack_left(x, windows, scr, left, cs):
    lane = lane_ids(Q)
    first = 2 * cs
    shifts = [(5 * (first + k2)) % 8 for k2 in range(2)]
    for n in range(2 * PG):
        for t in range(2):
            scr[n, t, 0:8, :] = jnp.zeros((8, 128), F32)
            scr[n, t, 72:80, :] = jnp.zeros((8, 128), F32)
    for r in range(RR):
        y = window(x, windows, r, LEFT_AT[r])
        for n in range(2 * PG):
            at = n * PG * Q
            e0, e1, e2 = (y[at + Q * p : at + Q * (p + 1)] for p in range(PG))
            low = jnp.where(lane < KP, e0[:, :128], e1[:, :128])
            high = jnp.where(lane < 2 * KP - 128, e1[:, 128:], e2[:, 128:])
            rows = pl.ds(shifts[n % 2] + r, Q, stride=RR)
            scr[n, 0, rows, :] = low
            scr[n, 1, rows, :] = high
    for n in range(2 * PG):
        for t in range(2):
            left[n // 2, first + n % 2, :, 128 * t : 128 * (t + 1)] = scr[n, t].astype(BF16)


def unpack_right(x, windows, compact, slots, cs):
    for u in range((RR + 1) // 2):
        y = window(x, windows, u, RIGHT_AT[u])
        for n, slot in enumerate(slots):
            for k2 in range(2):
                for p in range(PG):
                    at = n * ROWS + (k2 * PG + p) * Q
                    both = jnp.concatenate([y[at : at + Q, :128], y[at : at + Q, 128:]], axis=0)
                    compact[slot, 2 * cs + k2, p, 16 * u : 16 * u + 16, :] = both.astype(BF16)


def put_columns(colv, n, row):
    colv[pl.ds(n, 1), :] = row.astype(F32)[0:1].astype(jnp.int32)

def exchange_kernel(
    xc, xb, colv, left, compact, F, fscr, RX, LY, ZS, ZP, RF, LF, lscr, winl, winr,
    sa, ra, sb, rb, so, ro, sl, rl, s1, r1, s2, rs, rp, sf, rf, ls,
):
    row = lax.axis_index("row")
    col = lax.axis_index("col")
    z, yl, m, e = row // 4, (row // 2) % 2, row // 2, row % 2
    yh, x = col // 4, col % 4
    no, both, either = jnp.logical_not, jnp.logical_and, jnp.logical_or

    def remote(src, dst, send, recv, device):
        return pltpu.make_async_remote_copy(
            src_ref=src, dst_ref=dst, send_sem=send, recv_sem=recv, device_id=device, device_id_type=MESH
        )

    at_x = [(x + d) % 4 for d in range(4)]
    peers = {d: (row, yh * 4 + at_x[d]) for d in (1, 2, 3)}
    across = (row, (1 - yh) * 4 + x)
    sibling = (row + 1 - 2 * e, col)

    plan = {}
    for ci in range(2):
        C = x + 4 * ci
        for kind in range(2):
            b = e if kind == 0 else 1 - e
            u = yl - C - b + 16
            yl2, dz = u % 2, (u // 2) % 4
            stay_z = dz == 0
            stay_y = both(yh == ci, yl2 == yl)
            to_z = (z + dz) % 4
            plan[ci, kind] = dict(
                relay=both(no(stay_z), no(stay_y)),
                hop=(to_z * 4 + yl * 2 + e, col),
                hop_from=(((z - dz + 4) % 4) * 4 + yl * 2 + e, col),
                final=(jnp.where(stay_y, to_z, z) * 4 + yl2 * 2 + b, C),
                here=both(both(stay_z, stay_y), b == e),
            )
    senders = []
    ms = m + col + e
    for kind in range(2):
        es = e if kind == 0 else 1 - e
        for h in range(2):
            zs = jnp.where(both(yh == h, ms % 2 == yl), (ms // 2) % 4, z)
            device = (zs * 4 + (ms % 2) * 2 + es, h * 4 + x)
            senders.append((device, both(device[0] == row, device[1] == col)))

    barrier = pltpu.get_barrier_semaphore()

    def greet(device):
        pl.semaphore_signal(barrier, 1, device_id=device, device_id_type=MESH)

    for device in (peers[1], peers[2], peers[3], across, sibling):
        greet(device)
    count = jnp.int32(5)
    for v in plan.values():

        @pl.when(v["relay"])
        def _(v=v):
            greet(v["hop"])
            greet(v["hop_from"])

        @pl.when(no(v["here"]))
        def _(v=v):
            greet(v["final"])

        count = count + jnp.where(v["relay"], 2, 0) + jnp.where(v["here"], 0, 1)
    for device, mine in senders:

        @pl.when(no(mine))
        def _(device=device):
            greet(device)

        count = count + jnp.where(mine, 0, 1)

    pack(xc, xb, F, fscr)
    pl.semaphore_wait(barrier, count)

    def one(ref, i):
        return ref.at[pl.ds(i, 1)]

    def groups_at(place, ci):
        return 2 * place + 8 * ci

    def spread(d, ci):
        src = F.at[pl.ds(groups_at(at_x[d], ci), 2)]
        return remote(src, RX.at[ci, d - 1], sa.at[d - 1, ci], ra.at[d - 1, ci], peers[d])

    def cross(t):
        src = F.at[pl.ds((row + 8 * (1 - yh)) % 16 + 3 * t, 3)]
        return remote(src, LY.at[pl.ds(3 * t, 3)], sb.at[t], rb.at[t], across)

    def left_own(d, at):
        src = F.at[pl.ds((row + 2 * (yh * 4 + at_x[d])) % 16, 3)]
        return remote(src, LF.at[at], so.at[d - 1], ro.at[d - 1], peers[d])

    other = (1 - yh) * 4

    def left_across(d, at):
        return remote(LY.at[pl.ds(2 * at_x[d], 3)], LF.at[at], sl.at[d - 1], rl.at[d - 1], peers[d])

    def from_x(d):
        return yh * 4 + (x + 4 - d) % 4

    def right_src(ci, kind, d):
        if d == 0:
            return one(F, groups_at(x, ci) + e) if kind == 0 else F.at[pl.ds(groups_at(x, ci), 2)]
        return RX.at[ci, d - 1, pl.ds(e, 1)] if kind == 0 else RX.at[ci, d - 1]

    def right_dst(kind, d):
        return RF.at[pl.ds(3 * e, 1), from_x(d)] if kind == 0 else RF.at[pl.ds(1, 2), from_x(d)]

    def relay_at(ci, kind, d):
        return ZS.at[ci, d] if kind == 0 else ZP.at[ci, d]

    def arrive(kind, at):
        return rs.at[at] if kind == 0 else rp.at[at]

    def direct(ci, kind, d):
        to = plan[ci, kind]["final"]
        return remote(right_src(ci, kind, d), right_dst(kind, d), s1.at[ci, kind, d], arrive(kind, from_x(d)), to)

    def hop(ci, kind, d):
        to = plan[ci, kind]["hop"]
        return remote(right_src(ci, kind, d), relay_at(ci, kind, d), s1.at[ci, kind, d], r1.at[ci, kind, d], to)

    def last(ci, kind, d):
        to = plan[ci, kind]["final"]
        return remote(relay_at(ci, kind, d), right_dst(kind, d), s2.at[ci, kind, d], arrive(kind, from_x(d)), to)

    def stay(ci, d):
        return pltpu.make_async_copy(right_src(ci, 0, d), right_dst(0, d), ls.at[d])

    def right_start(ci, d):
        for kind in (1, 0):
            v = plan[ci, kind]

            @pl.when(v["relay"])
            def _():
                hop(ci, kind, d).start()

            if kind == 0:

                @pl.when(v["here"])
                def _():
                    stay(ci, d).start()

            @pl.when(no(either(v["relay"], v["here"])))
            def _():
                direct(ci, kind, d).start()

    def right_relay(ci, d):
        for kind in (1, 0):

            @pl.when(plan[ci, kind]["relay"])
            def _():
                hop(ci, kind, d).wait_recv()
                last(ci, kind, d).start()

    def right_sent(ci, d):
        for kind in (1, 0):
            v = plan[ci, kind]

            @pl.when(v["relay"])
            def _():
                hop(ci, kind, d).wait_send()
                last(ci, kind, d).wait_send()

            @pl.when(no(either(v["relay"], v["here"])))
            def _():
                direct(ci, kind, d).wait_send()

    any_here = either(plan[0, 0]["here"], plan[1, 0]["here"])

    def single_arrived(at):
        mine = both(any_here, at // 4 == yh)

        @pl.when(no(mine))
        def _():
            remote(F.at[pl.ds(0, 1)], RF.at[pl.ds(3 * e, 1), at], s1.at[0, 0, 0], rs.at[at], across).wait_recv()

        @pl.when(mine)
        def _():
            d = (x + 4 - at % 4) % 4
            pltpu.make_async_copy(F.at[pl.ds(0, 1)], RF.at[pl.ds(3 * e, 1), at], ls.at[d]).wait()

    def pair_arrived(at):
        remote(F.at[pl.ds(0, 2)], RF.at[pl.ds(1, 2), at], s1.at[0, 0, 0], rp.at[at], across).wait_recv()

    def hand(at):
        return remote(RF.at[pl.ds(1 + e, 1), at], RF.at[pl.ds(3 * e, 1), at], sf.at[at], rf.at[at], sibling)

    def handed(at):
        remote(F.at[pl.ds(0, 1)], RF.at[pl.ds(3 - 3 * e, 1), at], sf.at[at], rf.at[at], sibling).wait_recv()

    def take_left(packets, cs):
        for t in range(PG):
            put_columns(colv, 32 + cs * 3 + t, packets(t)[0:16, 512:640])
        rows = jnp.concatenate([packets(t) for t in range(PG)], axis=0)
        unpack_left(rows, winl, lscr, left, cs)

    def take_left_at(cs):
        take_left(lambda t: LF[cs, t], cs)

    def take_right(slots, cs):
        for slot in slots:
            put_columns(colv, slot * 8 + cs, RF[slot, cs, 0:16, 512:640])
        rows = jnp.concatenate([RF[slot, cs] for slot in slots], axis=0)
        unpack_right(rows, winr, compact, slots, cs)

    order = (2, 1, 3)
    for d in order:
        for ci in range(2):
            spread(d, ci).start()
    for t in range(3):
        cross(t).start()
    for ci in range(2):
        right_start(ci, 0)
    build_left_windows(winl)
    build_right_windows(winr)
    for n, d in enumerate(order):
        for ci in range(2):
            spread(d, ci).wait_recv()
            right_start(ci, d)
        left_own(d, col).start()
        for ci in range(2):
            right_relay(ci, 0 if n == 0 else order[n - 1])
    for t in range(3):
        cross(t).wait_recv()
    for d in order:
        left_across(d, other + x).start()
    for ci in range(2):
        right_relay(ci, order[2])
    take_left(lambda t: F[(row + 2 * col + t) % 16], col)
    take_left(lambda t: LY[2 * x + t], other + x)

    def place(n):
        d = n // 2
        d = jnp.where(d == 0, 0, jnp.where(d == 1, order[0], jnp.where(d == 2, order[1], order[2])))
        h = jnp.where(n % 2 == 0, yh, 1 - yh)
        return h * 4 + (x + 4 - d) % 4

    def pairs(n, _):
        at = place(n)
        pair_arrived(at)
        hand(at).start()
        take_right((1, 2), at)
        return 0

    lax.fori_loop(0, 8, pairs, 0)
    for d in order:
        left_own(d, from_x(d)).wait_recv()
        take_left_at(from_x(d))

    def singles(n, _):
        at = place(n)
        single_arrived(at)
        handed(at)
        take_right((0, 3), at)
        return 0

    lax.fori_loop(0, 8, singles, 0)
    for d in order:
        at = other + (x + 4 - d) % 4
        left_across(d, at).wait_recv()
        take_left_at(at)
    for d in order:
        for ci in range(2):
            spread(d, ci).wait_send()
        left_own(d, col).wait_send()
        left_across(d, other + x).wait_send()
    for t in range(3):
        cross(t).wait_send()
    for ci in range(2):
        for d in range(4):
            right_sent(ci, d)
    for at in range(8):
        hand(at).wait_send()


def exchange(x_cols, x_blocks):
    unit = (ROWS, LANES)
    return pl.pallas_call(
        exchange_kernel,
        out_shape=[
            jax.ShapeDtypeStruct((56, 128), jnp.int32),
            jax.ShapeDtypeStruct((3, BB, KP, 256), BF16),
            jax.ShapeDtypeStruct((4, BB, PG, KP, 128), BF16),
        ],
        in_specs=[pl.BlockSpec(memory_space=pltpu.SMEM), pl.BlockSpec(memory_space=pltpu.VMEM)],
        out_specs=[pl.BlockSpec(memory_space=pltpu.VMEM)] * 3,
        scratch_shapes=[
            pltpu.VMEM((KEPT,) + unit, BF16),
            pltpu.VMEM((LANES // 128, GROUPS * ROWS, 128), F32),
            pltpu.VMEM((2, 3, 2) + unit, BF16),
            pltpu.VMEM((9,) + unit, BF16),
            pltpu.VMEM((2, 4, 1) + unit, BF16),
            pltpu.VMEM((2, 4, 2) + unit, BF16),
            pltpu.VMEM((4, 8) + unit, BF16),
            pltpu.VMEM((8, 3) + unit, BF16),
            pltpu.VMEM((2 * PG, 2, KP, 128), F32),
            pltpu.VMEM((RR, 256, 256), BF16),
            pltpu.VMEM(((RR + 1) // 2, 256, 256), BF16),
        ]
        + [DMA(shape) for shape in ((3, 2), (3,), (3,), (3,), (2, 2, 4)) for _ in range(2)]
        + [DMA((2, 2, 4))]
        + [DMA((8,)) for _ in range(5)],
        compiler_params=pltpu.CompilerParams(
            collective_id=0, has_side_effects=True, vmem_limit_bytes=40 << 20
        ),
        name="exchange",
    )(x_cols, x_blocks)


def expand(compact, dense, cols, slot, at, k):
    lane = lane_ids(KP)
    shift = 16 * BLK - 1024 if slot >= 2 else 0
    dense[at, k] = jnp.zeros((KP, WIDE), BF16)
    for p in range(PG):
        start = shift + BLK * cols[slot * 8 + k // 2, TAIL + (k % 2) * PG + p]
        t = start // 128
        d = start - 128 * t
        y = pltpu.roll(compact[slot, k, p], d, 1)
        zero = jnp.zeros_like(y)
        low = pl.ds(pl.multiple_of(128 * t, 128), 128)
        high = pl.ds(pl.multiple_of(128 * t + 128, 128), 128)
        dense[at, k, :, low] += jnp.where(lane >= d, y, zero)
        dense[at, k, :, high] += jnp.where(lane < d, y, zero)


def product_kernel(cols, left, compact, out, even, odd, total, osem):
    half = Q * BLK

    def rows_of(h, v, j):
        rows = 64 if v < Q - 1 else half - 64 * v
        lanes = pl.ds(0, 1024) if j == 0 else pl.ds(1024, 2 * BB * BLK - 1024)
        src = total.at[h, pl.ds(64 * v, rows), lanes]
        dst = out.at[pl.ds(pl.multiple_of(half * h + 64 * v, 8), rows), lanes]
        return pltpu.make_async_copy(src, dst, osem.at[j, Q * h + v])

    def first(n, _):
        for k in (2 * n, 2 * n + 1):
            for slot in range(2):
                expand(compact, even, cols, slot, slot, k)
        return 0

    lax.fori_loop(0, BB // 8, lambda n, _: [first(4 * n + v, 0) for v in range(4)][-1], 0)
    for h in range(2):
        total[h, 0:8, :] = jnp.zeros((8, total.shape[2]), F32)

    def multiply(h, v, j, dense):
        i = Q * h + v
        ls = [left[j + s, i][:, : PG * KP] for s in range(2)]
        ks = [
            [cols[32 + (i // 2) * 3 + j + s, TAIL + (i % 2) * PG + p] for p in range(PG)] for s in range(2)
        ]
        base = BLK * v // 8 * 8
        for n in range(5):
            acc = None
            for s in range(2):
                w = jnp.concatenate([dense[s, k, :, 256 * n : 256 * (n + 1)] for k in ks[s]], axis=0)
                term = jnp.dot(ls[s], w, preferred_element_type=F32)
                acc = term if acc is None else acc + term
            lo = 1024 * j + 256 * n
            width = min(256, total.shape[2] - lo)
            lanes = slice(lo, lo + width)
            if j == 1 and n == 0:
                total[h, base : base + 80, lanes] += acc
            else:
                total[h, base : base + 8, lanes] += acc[0:8, :width]
                total[h, base + 8 : base + 80, lanes] = acc[8:80, :width]

    def second(h, _):
        for v in range(Q):
            multiply(h, v, 0, even)
            for slot in range(2, 4):
                expand(compact, odd, cols, slot, slot - 2, Q * h + v)
            rows_of(h, v, 0).start()
        return 0

    lax.fori_loop(0, 2, second, 0)

    def third(h, _):
        for v in range(Q):
            multiply(h, v, 1, odd)
            rows_of(h, v, 1).start()
        return 0

    lax.fori_loop(0, 2, third, 0)
    for j in range(2):
        for h in range(2):
            for v in range(Q):
                rows_of(h, v, j).wait()


def product(cols, left, compact):
    return pl.pallas_call(
        product_kernel,
        out_shape=jax.ShapeDtypeStruct((BB * BLK, 2 * BB * BLK), F32),
        in_specs=[pl.BlockSpec(memory_space=pltpu.SMEM)] + [pl.BlockSpec(memory_space=pltpu.VMEM)] * 2,
        out_specs=pl.BlockSpec(memory_space=pl.ANY),
        scratch_shapes=[
            pltpu.VMEM((2, BB, KP, WIDE), BF16),
            pltpu.VMEM((2, BB, KP, WIDE), BF16),
            pltpu.VMEM((2, Q * BLK + 8, 2 * BB * BLK), F32),
            DMA((2, BB)),
        ],
        compiler_params=pltpu.CompilerParams(vmem_limit_bytes=36 << 20),
        name="product",
    )(cols, left, compact)


def shards(x_blocks, x_cols):
    cols, left, compact = exchange(
        x_cols.transpose(2, 0, 1), x_blocks.transpose(0, 2, 1, 3).reshape(2 * PG, GROUPS, SIZE)
    )
    return product(cols, left, compact)


def solution(mesh):
    in_specs = (P(("row", "col"), None, None, None), P(("row", "col"), None, None))
    return jax.shard_map(shards, mesh=mesh, in_specs=in_specs, out_specs=P("row", "col"), check_vma=False)
```

```python
import jax
import jax.numpy as jnp
from jax import lax
from jax.experimental import pallas as pl
from jax.experimental.pallas import tpu as pltpu
from jax.sharding import PartitionSpec as P

BLK = 69
BB = 16
PG = 3
GROUPS = 16
Q = 8
RR = 9
CHUNK = RR * BLK
ROWS = 2 * PG * Q
LANES = 640
TAIL = CHUNK - 512
KP = 80
WIDE = 1280
KEPT = 25
SIZE = BLK * BLK
F32 = jnp.float32
BF16 = jnp.bfloat16
MESH = pl.DeviceIdType.MESH
DMA = pltpu.SemaphoreType.DMA


def lane_ids(rows):
    return lax.broadcasted_iota(jnp.int32, (rows, 128), 1)


def pack(cols_ref, x_ref, f_ref, scr):
    tiles = (SIZE + 127) // 128
    lane = lane_ids(Q)

    def some(n, _):
        for h in range(2):
            flat = x_ref[n, Q * h : Q * h + Q].astype(F32)
            parts = [flat[:, 128 * t : 128 * (t + 1)] for t in range(tiles - 1)]
            rest = jnp.zeros((Q, 128 * tiles - SIZE), F32)
            parts.append(jnp.concatenate([flat[:, 128 * (tiles - 1) : SIZE], rest], axis=1))
            parts.append(jnp.zeros((Q, 128), F32))
            for q in range(Q):
                for t in range(LANES // 128):
                    a, o = divmod(CHUNK * q + 128 * t, 128)
                    if a >= tiles:
                        piece = parts[tiles]
                    elif o:
                        piece = pltpu.roll(jnp.where(lane >= o, parts[a], parts[a + 1]), 128 - o, 1)
                    else:
                        piece = parts[a]
                    scr[t, pl.ds(Q * h * ROWS + n * Q + q, Q, stride=ROWS), :] = piece
        return 0

    lax.fori_loop(0, 2 * PG, some, 0)
    lane_all = lane_ids(ROWS)

    def group(g, _):
        at = pl.ds(pl.multiple_of(g * ROWS, 16), ROWS)
        for t in range(4):
            f_ref[g, :, 128 * t : 128 * (t + 1)] = scr[t, at, :].astype(BF16)
        tail = jnp.where(lane_all < TAIL, scr[4, at, :], 0.0)
        for k2 in range(2):
            for p in range(PG):
                value = cols_ref[p, k2, g].astype(F32)
                tail = jnp.where(lane_all == TAIL + k2 * PG + p, value, tail)
        f_ref[g, :, 512:640] = tail.astype(BF16)

        @pl.when(g < KEPT - GROUPS)
        def _():
            f_ref[g + GROUPS] = f_ref[g]

        return 0

    lax.fori_loop(0, GROUPS, group, 0)


LEFT_AT = [min(BLK * r // 128, 3) for r in range(RR)]
RIGHT_AT = [min(2 * BLK * u // 128, 3) for u in range((RR + 1) // 2)]


def build_left_windows(ref):
    source = lax.broadcasted_iota(jnp.int32, (256, 256), 0)
    target = lax.broadcasted_iota(jnp.int32, (256, 256), 1)
    place = target - KP * (target // KP)
    q = place - Q * (place // Q)
    wanted = jnp.where(target < PG * KP, RR * q + place // Q, BLK)
    wanted = jnp.where(place < Q * RR, wanted, BLK)
    gap = jnp.where(wanted < BLK, source - wanted, -1024)

    def one(r, _):
        start = BLK * r - 128 * jnp.minimum(BLK * r // 128, 3)
        ref[r] = jnp.where(gap == start, 1.0, 0.0).astype(BF16)
        return 0

    lax.fori_loop(0, RR, one, 0)


def build_right_windows(ref):
    source = lax.broadcasted_iota(jnp.int32, (256, 256), 0)
    target = lax.broadcasted_iota(jnp.int32, (256, 256), 1)
    half = target // 128
    b = target - 128 * half
    gap = jnp.where(b < BLK, source - b - BLK * half, -1024)

    def one(u, _):
        start = 2 * BLK * u - 128 * jnp.minimum(2 * BLK * u // 128, 3)
        keep = jnp.logical_or(half == 0, u < RR // 2)
        ref[u] = jnp.where(jnp.logical_and(gap == start, keep), 1.0, 0.0).astype(BF16)
        return 0

    lax.fori_loop(0, (RR + 1) // 2, one, 0)


def window(x, ref, n, at):
    return jnp.dot(x[:, 128 * at : 128 * at + 256], ref[n], preferred_element_type=F32)


def unpack_left(x, windows, scr, left, cs):
    lane = lane_ids(Q)
    first = 2 * cs
    shifts = [(5 * (first + k2)) % 8 for k2 in range(2)]
    for n in range(2 * PG):
        for t in range(2):
            scr[n, t, 0:8, :] = jnp.zeros((8, 128), F32)
            scr[n, t, 72:80, :] = jnp.zeros((8, 128), F32)
    for r in range(RR):
        y = window(x, windows, r, LEFT_AT[r])
        for n in range(2 * PG):
            at = n * PG * Q
            e0, e1, e2 = (y[at + Q * p : at + Q * (p + 1)] for p in range(PG))
            low = jnp.where(lane < KP, e0[:, :128], e1[:, :128])
            high = jnp.where(lane < 2 * KP - 128, e1[:, 128:], e2[:, 128:])
            rows = pl.ds(shifts[n % 2] + r, Q, stride=RR)
            scr[n, 0, rows, :] = low
            scr[n, 1, rows, :] = high
    for n in range(2 * PG):
        for t in range(2):
            left[n // 2, first + n % 2, :, 128 * t : 128 * (t + 1)] = scr[n, t].astype(BF16)


def unpack_right(x, windows, compact, slots, cs):
    for u in range((RR + 1) // 2):
        y = window(x, windows, u, RIGHT_AT[u])
        for n, slot in enumerate(slots):
            for k2 in range(2):
                for p in range(PG):
                    at = n * ROWS + (k2 * PG + p) * Q
                    both = jnp.concatenate([y[at : at + Q, :128], y[at : at + Q, 128:]], axis=0)
                    compact[slot, 2 * cs + k2, p, 16 * u : 16 * u + 16, :] = both.astype(BF16)


def put_columns(colv, n, row):
    colv[pl.ds(n, 1), :] = row.astype(F32)[0:1].astype(jnp.int32)

def exchange_kernel(
    xc, xb, colv, left, compact, F, fscr, RX, LY, ZS, ZP, RF, LF, lscr, winl, winr,
    sa, ra, sb, rb, so, ro, sl, rl, s1, r1, s2, rs, rp, sf, rf, ls,
):
    row = lax.axis_index("row")
    col = lax.axis_index("col")
    z, yl, m, e = row // 4, (row // 2) % 2, row // 2, row % 2
    yh, x = col // 4, col % 4
    no, both, either = jnp.logical_not, jnp.logical_and, jnp.logical_or

    def remote(src, dst, send, recv, device):
        return pltpu.make_async_remote_copy(
            src_ref=src, dst_ref=dst, send_sem=send, recv_sem=recv, device_id=device, device_id_type=MESH
        )

    at_x = [(x + d) % 4 for d in range(4)]
    peers = {d: (row, yh * 4 + at_x[d]) for d in (1, 2, 3)}
    across = (row, (1 - yh) * 4 + x)
    sibling = (row + 1 - 2 * e, col)

    plan = {}
    for ci in range(2):
        C = x + 4 * ci
        for kind in range(2):
            b = e if kind == 0 else 1 - e
            u = yl - C - b + 16
            yl2, dz = u % 2, (u // 2) % 4
            stay_z = dz == 0
            stay_y = both(yh == ci, yl2 == yl)
            to_z = (z + dz) % 4
            plan[ci, kind] = dict(
                relay=both(no(stay_z), no(stay_y)),
                hop=(to_z * 4 + yl * 2 + e, col),
                hop_from=(((z - dz + 4) % 4) * 4 + yl * 2 + e, col),
                final=(jnp.where(stay_y, to_z, z) * 4 + yl2 * 2 + b, C),
                here=both(both(stay_z, stay_y), b == e),
            )
    senders = []
    ms = m + col + e
    for kind in range(2):
        es = e if kind == 0 else 1 - e
        for h in range(2):
            zs = jnp.where(both(yh == h, ms % 2 == yl), (ms // 2) % 4, z)
            device = (zs * 4 + (ms % 2) * 2 + es, h * 4 + x)
            senders.append((device, both(device[0] == row, device[1] == col)))

    barrier = pltpu.get_barrier_semaphore()

    def greet(device):
        pl.semaphore_signal(barrier, 1, device_id=device, device_id_type=MESH)

    for device in (peers[1], peers[2], peers[3], across, sibling):
        greet(device)
    count = jnp.int32(5)
    for v in plan.values():

        @pl.when(v["relay"])
        def _(v=v):
            greet(v["hop"])
            greet(v["hop_from"])

        @pl.when(no(v["here"]))
        def _(v=v):
            greet(v["final"])

        count = count + jnp.where(v["relay"], 2, 0) + jnp.where(v["here"], 0, 1)
    for device, mine in senders:

        @pl.when(no(mine))
        def _(device=device):
            greet(device)

        count = count + jnp.where(mine, 0, 1)

    pack(xc, xb, F, fscr)
    pl.semaphore_wait(barrier, count)

    def one(ref, i):
        return ref.at[pl.ds(i, 1)]

    def groups_at(place, ci):
        return 2 * place + 8 * ci

    def spread(d, ci):
        src = F.at[pl.ds(groups_at(at_x[d], ci), 2)]
        return remote(src, RX.at[ci, d - 1], sa.at[d - 1, ci], ra.at[d - 1, ci], peers[d])

    def cross(t):
        src = F.at[pl.ds((row + 8 * (1 - yh)) % 16 + 3 * t, 3)]
        return remote(src, LY.at[pl.ds(3 * t, 3)], sb.at[t], rb.at[t], across)

    def left_own(d, at):
        src = F.at[pl.ds((row + 2 * (yh * 4 + at_x[d])) % 16, 3)]
        return remote(src, LF.at[at], so.at[d - 1], ro.at[d - 1], peers[d])

    other = (1 - yh) * 4

    def left_across(d, at):
        return remote(LY.at[pl.ds(2 * at_x[d], 3)], LF.at[at], sl.at[d - 1], rl.at[d - 1], peers[d])

    def from_x(d):
        return yh * 4 + (x + 4 - d) % 4

    def right_src(ci, kind, d):
        if d == 0:
            return one(F, groups_at(x, ci) + e) if kind == 0 else F.at[pl.ds(groups_at(x, ci), 2)]
        return RX.at[ci, d - 1, pl.ds(e, 1)] if kind == 0 else RX.at[ci, d - 1]

    def right_dst(kind, d):
        return RF.at[pl.ds(3 * e, 1), from_x(d)] if kind == 0 else RF.at[pl.ds(1, 2), from_x(d)]

    def relay_at(ci, kind, d):
        return ZS.at[ci, d] if kind == 0 else ZP.at[ci, d]

    def arrive(kind, at):
        return rs.at[at] if kind == 0 else rp.at[at]

    def direct(ci, kind, d):
        to = plan[ci, kind]["final"]
        return remote(right_src(ci, kind, d), right_dst(kind, d), s1.at[ci, kind, d], arrive(kind, from_x(d)), to)

    def hop(ci, kind, d):
        to = plan[ci, kind]["hop"]
        return remote(right_src(ci, kind, d), relay_at(ci, kind, d), s1.at[ci, kind, d], r1.at[ci, kind, d], to)

    def last(ci, kind, d):
        to = plan[ci, kind]["final"]
        return remote(relay_at(ci, kind, d), right_dst(kind, d), s2.at[ci, kind, d], arrive(kind, from_x(d)), to)

    def stay(ci, d):
        return pltpu.make_async_copy(right_src(ci, 0, d), right_dst(0, d), ls.at[d])

    def right_start(ci, d):
        for kind in (1, 0):
            v = plan[ci, kind]

            @pl.when(v["relay"])
            def _():
                hop(ci, kind, d).start()

            if kind == 0:

                @pl.when(v["here"])
                def _():
                    stay(ci, d).start()

            @pl.when(no(either(v["relay"], v["here"])))
            def _():
                direct(ci, kind, d).start()

    def right_relay(ci, d):
        for kind in (1, 0):

            @pl.when(plan[ci, kind]["relay"])
            def _():
                hop(ci, kind, d).wait_recv()
                last(ci, kind, d).start()

    def right_sent(ci, d):
        for kind in (1, 0):
            v = plan[ci, kind]

            @pl.when(v["relay"])
            def _():
                hop(ci, kind, d).wait_send()
                last(ci, kind, d).wait_send()

            @pl.when(no(either(v["relay"], v["here"])))
            def _():
                direct(ci, kind, d).wait_send()

    any_here = either(plan[0, 0]["here"], plan[1, 0]["here"])

    def single_arrived(at):
        mine = both(any_here, at // 4 == yh)

        @pl.when(no(mine))
        def _():
            remote(F.at[pl.ds(0, 1)], RF.at[pl.ds(3 * e, 1), at], s1.at[0, 0, 0], rs.at[at], across).wait_recv()

        @pl.when(mine)
        def _():
            d = (x + 4 - at % 4) % 4
            pltpu.make_async_copy(F.at[pl.ds(0, 1)], RF.at[pl.ds(3 * e, 1), at], ls.at[d]).wait()

    def pair_arrived(at):
        remote(F.at[pl.ds(0, 2)], RF.at[pl.ds(1, 2), at], s1.at[0, 0, 0], rp.at[at], across).wait_recv()

    def hand(at):
        return remote(RF.at[pl.ds(1 + e, 1), at], RF.at[pl.ds(3 * e, 1), at], sf.at[at], rf.at[at], sibling)

    def handed(at):
        remote(F.at[pl.ds(0, 1)], RF.at[pl.ds(3 - 3 * e, 1), at], sf.at[at], rf.at[at], sibling).wait_recv()

    def take_left(packets, cs):
        for t in range(PG):
            put_columns(colv, 32 + cs * 3 + t, packets(t)[0:16, 512:640])
        rows = jnp.concatenate([packets(t) for t in range(PG)], axis=0)
        unpack_left(rows, winl, lscr, left, cs)

    def take_left_at(cs):
        take_left(lambda t: LF[cs, t], cs)

    def take_right(slots, cs):
        for slot in slots:
            put_columns(colv, slot * 8 + cs, RF[slot, cs, 0:16, 512:640])
        rows = jnp.concatenate([RF[slot, cs] for slot in slots], axis=0)
        unpack_right(rows, winr, compact, slots, cs)

    order = (2, 1, 3)
    for d in order:
        for ci in range(2):
            spread(d, ci).start()
    for t in range(3):
        cross(t).start()
    for ci in range(2):
        right_start(ci, 0)
    for d in order:
        left_own(d, col).start()
    for ci in range(2):
        right_relay(ci, 0)
    build_left_windows(winl)
    build_right_windows(winr)
    for n, d in enumerate(order):
        for ci in range(2):
            spread(d, ci).wait_recv()
            right_start(ci, d)
        for ci in range(2):
            if n:
                right_relay(ci, order[n - 1])
    for t in range(3):
        cross(t).wait_recv()
    for d in order:
        left_across(d, other + x).start()
    for ci in range(2):
        right_relay(ci, order[2])
    take_left(lambda t: F[(row + 2 * col + t) % 16], col)
    take_left(lambda t: LY[2 * x + t], other + x)

    def place(n):
        d = n // 2
        d = jnp.where(d == 0, 0, jnp.where(d == 1, order[0], jnp.where(d == 2, order[1], order[2])))
        h = jnp.where(n % 2 == 0, yh, 1 - yh)
        return h * 4 + (x + 4 - d) % 4

    def pairs(n, _):
        at = place(n)
        pair_arrived(at)
        hand(at).start()
        take_right((1, 2), at)
        return 0

    lax.fori_loop(0, 8, pairs, 0)
    for d in order:
        left_own(d, from_x(d)).wait_recv()
        take_left_at(from_x(d))

    def singles(n, _):
        at = place(n)
        single_arrived(at)
        handed(at)
        take_right((0, 3), at)
        return 0

    lax.fori_loop(0, 8, singles, 0)
    for d in order:
        at = other + (x + 4 - d) % 4
        left_across(d, at).wait_recv()
        take_left_at(at)
    for d in order:
        for ci in range(2):
            spread(d, ci).wait_send()
        left_own(d, col).wait_send()
        left_across(d, other + x).wait_send()
    for t in range(3):
        cross(t).wait_send()
    for ci in range(2):
        for d in range(4):
            right_sent(ci, d)
    for at in range(8):
        hand(at).wait_send()


def exchange(x_cols, x_blocks):
    unit = (ROWS, LANES)
    return pl.pallas_call(
        exchange_kernel,
        out_shape=[
            jax.ShapeDtypeStruct((56, 128), jnp.int32),
            jax.ShapeDtypeStruct((3, BB, KP, 256), BF16),
            jax.ShapeDtypeStruct((4, BB, PG, KP, 128), BF16),
        ],
        in_specs=[pl.BlockSpec(memory_space=pltpu.SMEM), pl.BlockSpec(memory_space=pltpu.VMEM)],
        out_specs=[pl.BlockSpec(memory_space=pltpu.VMEM)] * 3,
        scratch_shapes=[
            pltpu.VMEM((KEPT,) + unit, BF16),
            pltpu.VMEM((LANES // 128, GROUPS * ROWS, 128), F32),
            pltpu.VMEM((2, 3, 2) + unit, BF16),
            pltpu.VMEM((9,) + unit, BF16),
            pltpu.VMEM((2, 4, 1) + unit, BF16),
            pltpu.VMEM((2, 4, 2) + unit, BF16),
            pltpu.VMEM((4, 8) + unit, BF16),
            pltpu.VMEM((8, 3) + unit, BF16),
            pltpu.VMEM((2 * PG, 2, KP, 128), F32),
            pltpu.VMEM((RR, 256, 256), BF16),
            pltpu.VMEM(((RR + 1) // 2, 256, 256), BF16),
        ]
        + [DMA(shape) for shape in ((3, 2), (3,), (3,), (3,), (2, 2, 4)) for _ in range(2)]
        + [DMA((2, 2, 4))]
        + [DMA((8,)) for _ in range(5)],
        compiler_params=pltpu.CompilerParams(
            collective_id=0, has_side_effects=True, vmem_limit_bytes=40 << 20
        ),
        name="exchange",
    )(x_cols, x_blocks)


def expand(compact, dense, cols, slot, at, k):
    lane = lane_ids(KP)
    shift = 16 * BLK - 1024 if slot >= 2 else 0
    dense[at, k] = jnp.zeros((KP, WIDE), BF16)
    for p in range(PG):
        start = shift + BLK * cols[slot * 8 + k // 2, TAIL + (k % 2) * PG + p]
        t = start // 128
        d = start - 128 * t
        y = pltpu.roll(compact[slot, k, p], d, 1)
        zero = jnp.zeros_like(y)
        low = pl.ds(pl.multiple_of(128 * t, 128), 128)
        high = pl.ds(pl.multiple_of(128 * t + 128, 128), 128)
        dense[at, k, :, low] += jnp.where(lane >= d, y, zero)
        dense[at, k, :, high] += jnp.where(lane < d, y, zero)


def product_kernel(cols, left, compact, out, even, odd, total, osem):
    half = Q * BLK

    def rows_of(h, v, j):
        rows = 64 if v < Q - 1 else half - 64 * v
        lanes = pl.ds(0, 1024) if j == 0 else pl.ds(1024, 2 * BB * BLK - 1024)
        src = total.at[h, pl.ds(64 * v, rows), lanes]
        dst = out.at[pl.ds(pl.multiple_of(half * h + 64 * v, 8), rows), lanes]
        return pltpu.make_async_copy(src, dst, osem.at[j, Q * h + v])

    def first(n, _):
        for k in (2 * n, 2 * n + 1):
            for slot in range(2):
                expand(compact, even, cols, slot, slot, k)
        return 0

    lax.fori_loop(0, BB // 8, lambda n, _: [first(4 * n + v, 0) for v in range(4)][-1], 0)
    for h in range(2):
        total[h, 0:8, :] = jnp.zeros((8, total.shape[2]), F32)

    def multiply(h, v, j, dense):
        i = Q * h + v
        ls = [left[j + s, i][:, : PG * KP] for s in range(2)]
        ks = [
            [cols[32 + (i // 2) * 3 + j + s, TAIL + (i % 2) * PG + p] for p in range(PG)] for s in range(2)
        ]
        base = BLK * v // 8 * 8
        for n in range(5):
            acc = None
            for s in range(2):
                w = jnp.concatenate([dense[s, k, :, 256 * n : 256 * (n + 1)] for k in ks[s]], axis=0)
                term = jnp.dot(ls[s], w, preferred_element_type=F32)
                acc = term if acc is None else acc + term
            lo = 1024 * j + 256 * n
            width = min(256, total.shape[2] - lo)
            lanes = slice(lo, lo + width)
            if j == 1 and n == 0:
                total[h, base : base + 80, lanes] += acc
            else:
                total[h, base : base + 8, lanes] += acc[0:8, :width]
                total[h, base + 8 : base + 80, lanes] = acc[8:80, :width]

    def second(h, _):
        for v in range(Q):
            multiply(h, v, 0, even)
            for slot in range(2, 4):
                expand(compact, odd, cols, slot, slot - 2, Q * h + v)
            rows_of(h, v, 0).start()
        return 0

    lax.fori_loop(0, 2, second, 0)

    def third(h, _):
        for v in range(Q):
            multiply(h, v, 1, odd)
            rows_of(h, v, 1).start()
        return 0

    lax.fori_loop(0, 2, third, 0)
    for j in range(2):
        for h in range(2):
            for v in range(Q):
                rows_of(h, v, j).wait()


def product(cols, left, compact):
    return pl.pallas_call(
        product_kernel,
        out_shape=jax.ShapeDtypeStruct((BB * BLK, 2 * BB * BLK), F32),
        in_specs=[pl.BlockSpec(memory_space=pltpu.SMEM)] + [pl.BlockSpec(memory_space=pltpu.VMEM)] * 2,
        out_specs=pl.BlockSpec(memory_space=pl.ANY),
        scratch_shapes=[
            pltpu.VMEM((2, BB, KP, WIDE), BF16),
            pltpu.VMEM((2, BB, KP, WIDE), BF16),
            pltpu.VMEM((2, Q * BLK + 8, 2 * BB * BLK), F32),
            DMA((2, BB)),
        ],
        compiler_params=pltpu.CompilerParams(vmem_limit_bytes=36 << 20),
        name="product",
    )(cols, left, compact)


def shards(x_blocks, x_cols):
    cols, left, compact = exchange(
        x_cols.transpose(2, 0, 1), x_blocks.transpose(0, 2, 1, 3).reshape(2 * PG, GROUPS, SIZE)
    )
    return product(cols, left, compact)


def solution(mesh):
    in_specs = (P(("row", "col"), None, None, None), P(("row", "col"), None, None))
    return jax.shard_map(shards, mesh=mesh, in_specs=in_specs, out_specs=P("row", "col"), check_vma=False)
```

```python
import jax
import jax.numpy as jnp
from jax import lax
from jax.experimental import pallas as pl
from jax.experimental.pallas import tpu as pltpu
from jax.sharding import PartitionSpec as P

BLK = 69
BB = 16
PG = 3
GROUPS = 16
Q = 8
RR = 9
CHUNK = RR * BLK
ROWS = 2 * PG * Q
LANES = 640
TAIL = CHUNK - 512
KP = 80
WIDE = 1280
KEPT = 25
SIZE = BLK * BLK
F32 = jnp.float32
BF16 = jnp.bfloat16
MESH = pl.DeviceIdType.MESH
DMA = pltpu.SemaphoreType.DMA


def lane_ids(rows):
    return lax.broadcasted_iota(jnp.int32, (rows, 128), 1)


def pack(cols_ref, x_ref, f_ref, scr):
    tiles = (SIZE + 127) // 128
    lane = lane_ids(Q)

    def some(n, _):
        for h in range(2):
            flat = x_ref[n, Q * h : Q * h + Q].astype(F32)
            parts = [flat[:, 128 * t : 128 * (t + 1)] for t in range(tiles - 1)]
            rest = jnp.zeros((Q, 128 * tiles - SIZE), F32)
            parts.append(jnp.concatenate([flat[:, 128 * (tiles - 1) : SIZE], rest], axis=1))
            parts.append(jnp.zeros((Q, 128), F32))
            for q in range(Q):
                for t in range(LANES // 128):
                    a, o = divmod(CHUNK * q + 128 * t, 128)
                    if a >= tiles:
                        piece = parts[tiles]
                    elif o:
                        piece = pltpu.roll(jnp.where(lane >= o, parts[a], parts[a + 1]), 128 - o, 1)
                    else:
                        piece = parts[a]
                    scr[t, pl.ds(Q * h * ROWS + n * Q + q, Q, stride=ROWS), :] = piece
        return 0

    lax.fori_loop(0, 2 * PG, some, 0)
    lane_all = lane_ids(ROWS)

    def group(g, _):
        at = pl.ds(pl.multiple_of(g * ROWS, 16), ROWS)
        for t in range(4):
            f_ref[g, :, 128 * t : 128 * (t + 1)] = scr[t, at, :].astype(BF16)
        tail = jnp.where(lane_all < TAIL, scr[4, at, :], 0.0)
        for k2 in range(2):
            for p in range(PG):
                value = cols_ref[p, k2, g].astype(F32)
                tail = jnp.where(lane_all == TAIL + k2 * PG + p, value, tail)
        f_ref[g, :, 512:640] = tail.astype(BF16)

        @pl.when(g < KEPT - GROUPS)
        def _():
            f_ref[g + GROUPS] = f_ref[g]

        return 0

    lax.fori_loop(0, GROUPS, group, 0)


LEFT_AT = [min(BLK * r // 128, 3) for r in range(RR)]
RIGHT_AT = [min(2 * BLK * u // 128, 3) for u in range((RR + 1) // 2)]


def build_left_windows(ref):
    source = lax.broadcasted_iota(jnp.int32, (256, 256), 0)
    target = lax.broadcasted_iota(jnp.int32, (256, 256), 1)
    place = target - KP * (target // KP)
    q = place - Q * (place // Q)
    wanted = jnp.where(target < PG * KP, RR * q + place // Q, BLK)
    wanted = jnp.where(place < Q * RR, wanted, BLK)
    gap = jnp.where(wanted < BLK, source - wanted, -1024)

    def one(r, _):
        start = BLK * r - 128 * jnp.minimum(BLK * r // 128, 3)
        ref[r] = jnp.where(gap == start, 1.0, 0.0).astype(BF16)
        return 0

    lax.fori_loop(0, RR, one, 0)


def build_right_windows(ref):
    source = lax.broadcasted_iota(jnp.int32, (256, 256), 0)
    target = lax.broadcasted_iota(jnp.int32, (256, 256), 1)
    half = target // 128
    b = target - 128 * half
    gap = jnp.where(b < BLK, source - b - BLK * half, -1024)

    def one(u, _):
        start = 2 * BLK * u - 128 * jnp.minimum(2 * BLK * u // 128, 3)
        keep = jnp.logical_or(half == 0, u < RR // 2)
        ref[u] = jnp.where(jnp.logical_and(gap == start, keep), 1.0, 0.0).astype(BF16)
        return 0

    lax.fori_loop(0, (RR + 1) // 2, one, 0)


def window(x, ref, n, at):
    return jnp.dot(x[:, 128 * at : 128 * at + 256], ref[n], preferred_element_type=F32)


def unpack_left(x, windows, scr, left, cs):
    lane = lane_ids(Q)
    first = 2 * cs
    shifts = [(5 * (first + k2)) % 8 for k2 in range(2)]
    for n in range(2 * PG):
        for t in range(2):
            scr[n, t, 0:8, :] = jnp.zeros((8, 128), F32)
            scr[n, t, 72:80, :] = jnp.zeros((8, 128), F32)
    for r in range(RR):
        y = window(x, windows, r, LEFT_AT[r])
        for n in range(2 * PG):
            at = n * PG * Q
            e0, e1, e2 = (y[at + Q * p : at + Q * (p + 1)] for p in range(PG))
            low = jnp.where(lane < KP, e0[:, :128], e1[:, :128])
            high = jnp.where(lane < 2 * KP - 128, e1[:, 128:], e2[:, 128:])
            rows = pl.ds(shifts[n % 2] + r, Q, stride=RR)
            scr[n, 0, rows, :] = low
            scr[n, 1, rows, :] = high
    for n in range(2 * PG):
        for t in range(2):
            left[n // 2, first + n % 2, :, 128 * t : 128 * (t + 1)] = scr[n, t, 0:KP, :].astype(BF16)


def unpack_right(x, windows, compact, slots, cs):
    for u in range((RR + 1) // 2):
        y = window(x, windows, u, RIGHT_AT[u])
        for n, slot in enumerate(slots):
            for k2 in range(2):
                for p in range(PG):
                    at = n * ROWS + (k2 * PG + p) * Q
                    both = jnp.concatenate([y[at : at + Q, :128], y[at : at + Q, 128:]], axis=0)
                    compact[slot, 2 * cs + k2, p, 16 * u : 16 * u + 16, :] = both.astype(BF16)


def put_columns(colv, n, row):
    colv[pl.ds(n, 1), :] = row.astype(F32)[0:1].astype(jnp.int32)

def exchange_kernel(
    xc, xb, colv, left, compact, F, fscr, RX, LY, ZS, ZP, RF, LF, lscr, winl, winr,
    sa, ra, sb, rb, so, ro, sl, rl, s1, r1, s2, rs, rp, sf, rf, ls,
):
    row = lax.axis_index("row")
    col = lax.axis_index("col")
    z, yl, m, e = row // 4, (row // 2) % 2, row // 2, row % 2
    yh, x = col // 4, col % 4
    no, both, either = jnp.logical_not, jnp.logical_and, jnp.logical_or

    def remote(src, dst, send, recv, device):
        return pltpu.make_async_remote_copy(
            src_ref=src, dst_ref=dst, send_sem=send, recv_sem=recv, device_id=device, device_id_type=MESH
        )

    at_x = [(x + d) % 4 for d in range(4)]
    peers = {d: (row, yh * 4 + at_x[d]) for d in (1, 2, 3)}
    across = (row, (1 - yh) * 4 + x)
    sibling = (row + 1 - 2 * e, col)

    plan = {}
    for ci in range(2):
        C = x + 4 * ci
        for kind in range(2):
            b = e if kind == 0 else 1 - e
            u = yl - C - b + 16
            yl2, dz = u % 2, (u // 2) % 4
            stay_z = dz == 0
            stay_y = both(yh == ci, yl2 == yl)
            to_z = (z + dz) % 4
            plan[ci, kind] = dict(
                relay=both(no(stay_z), no(stay_y)),
                hop=(to_z * 4 + yl * 2 + e, col),
                hop_from=(((z - dz + 4) % 4) * 4 + yl * 2 + e, col),
                final=(jnp.where(stay_y, to_z, z) * 4 + yl2 * 2 + b, C),
                here=both(both(stay_z, stay_y), b == e),
            )
    senders = []
    ms = m + col + e
    for kind in range(2):
        es = e if kind == 0 else 1 - e
        for h in range(2):
            zs = jnp.where(both(yh == h, ms % 2 == yl), (ms // 2) % 4, z)
            device = (zs * 4 + (ms % 2) * 2 + es, h * 4 + x)
            senders.append((device, both(device[0] == row, device[1] == col)))

    barrier = pltpu.get_barrier_semaphore()

    def greet(device):
        pl.semaphore_signal(barrier, 1, device_id=device, device_id_type=MESH)

    for device in (peers[1], peers[2], peers[3], across, sibling):
        greet(device)
    count = jnp.int32(5)
    for v in plan.values():

        @pl.when(v["relay"])
        def _(v=v):
            greet(v["hop"])
            greet(v["hop_from"])

        @pl.when(no(v["here"]))
        def _(v=v):
            greet(v["final"])

        count = count + jnp.where(v["relay"], 2, 0) + jnp.where(v["here"], 0, 1)
    for device, mine in senders:

        @pl.when(no(mine))
        def _(device=device):
            greet(device)

        count = count + jnp.where(mine, 0, 1)

    pack(xc, xb, F, fscr)
    pl.semaphore_wait(barrier, count)

    def one(ref, i):
        return ref.at[pl.ds(i, 1)]

    def groups_at(place, ci):
        return 2 * place + 8 * ci

    def spread(d, ci):
        src = F.at[pl.ds(groups_at(at_x[d], ci), 2)]
        return remote(src, RX.at[ci, d - 1], sa.at[d - 1, ci], ra.at[d - 1, ci], peers[d])

    def cross(t):
        src = F.at[pl.ds((row + 8 * (1 - yh)) % 16 + 3 * t, 3)]
        return remote(src, LY.at[pl.ds(3 * t, 3)], sb.at[t], rb.at[t], across)

    def left_own(d, at):
        src = F.at[pl.ds((row + 2 * (yh * 4 + at_x[d])) % 16, 3)]
        return remote(src, LF.at[at], so.at[d - 1], ro.at[d - 1], peers[d])

    other = (1 - yh) * 4

    def left_across(d, at):
        return remote(LY.at[pl.ds(2 * at_x[d], 3)], LF.at[at], sl.at[d - 1], rl.at[d - 1], peers[d])

    def from_x(d):
        return yh * 4 + (x + 4 - d) % 4

    def right_src(ci, kind, d):
        if d == 0:
            return one(F, groups_at(x, ci) + e) if kind == 0 else F.at[pl.ds(groups_at(x, ci), 2)]
        return RX.at[ci, d - 1, pl.ds(e, 1)] if kind == 0 else RX.at[ci, d - 1]

    def right_dst(kind, d):
        return RF.at[pl.ds(3 * e, 1), from_x(d)] if kind == 0 else RF.at[pl.ds(1, 2), from_x(d)]

    def relay_at(ci, kind, d):
        return ZS.at[ci, d] if kind == 0 else ZP.at[ci, d]

    def arrive(kind, at):
        return rs.at[at] if kind == 0 else rp.at[at]

    def direct(ci, kind, d):
        to = plan[ci, kind]["final"]
        return remote(right_src(ci, kind, d), right_dst(kind, d), s1.at[ci, kind, d], arrive(kind, from_x(d)), to)

    def hop(ci, kind, d):
        to = plan[ci, kind]["hop"]
        return remote(right_src(ci, kind, d), relay_at(ci, kind, d), s1.at[ci, kind, d], r1.at[ci, kind, d], to)

    def last(ci, kind, d):
        to = plan[ci, kind]["final"]
        return remote(relay_at(ci, kind, d), right_dst(kind, d), s2.at[ci, kind, d], arrive(kind, from_x(d)), to)

    def stay(ci, d):
        return pltpu.make_async_copy(right_src(ci, 0, d), right_dst(0, d), ls.at[d])

    def right_start(ci, d):
        for kind in (1, 0):
            v = plan[ci, kind]

            @pl.when(v["relay"])
            def _():
                hop(ci, kind, d).start()

            if kind == 0:

                @pl.when(v["here"])
                def _():
                    stay(ci, d).start()

            @pl.when(no(either(v["relay"], v["here"])))
            def _():
                direct(ci, kind, d).start()

    def right_relay(ci, d):
        for kind in (1, 0):

            @pl.when(plan[ci, kind]["relay"])
            def _():
                hop(ci, kind, d).wait_recv()
                last(ci, kind, d).start()

    def right_sent(ci, d):
        for kind in (1, 0):
            v = plan[ci, kind]

            @pl.when(v["relay"])
            def _():
                hop(ci, kind, d).wait_send()
                last(ci, kind, d).wait_send()

            @pl.when(no(either(v["relay"], v["here"])))
            def _():
                direct(ci, kind, d).wait_send()

    any_here = either(plan[0, 0]["here"], plan[1, 0]["here"])

    def single_arrived(at):
        mine = both(any_here, at // 4 == yh)

        @pl.when(no(mine))
        def _():
            remote(F.at[pl.ds(0, 1)], RF.at[pl.ds(3 * e, 1), at], s1.at[0, 0, 0], rs.at[at], across).wait_recv()

        @pl.when(mine)
        def _():
            d = (x + 4 - at % 4) % 4
            pltpu.make_async_copy(F.at[pl.ds(0, 1)], RF.at[pl.ds(3 * e, 1), at], ls.at[d]).wait()

    def pair_arrived(at):
        remote(F.at[pl.ds(0, 2)], RF.at[pl.ds(1, 2), at], s1.at[0, 0, 0], rp.at[at], across).wait_recv()

    def hand(at):
        return remote(RF.at[pl.ds(1 + e, 1), at], RF.at[pl.ds(3 * e, 1), at], sf.at[at], rf.at[at], sibling)

    def handed(at):
        remote(F.at[pl.ds(0, 1)], RF.at[pl.ds(3 - 3 * e, 1), at], sf.at[at], rf.at[at], sibling).wait_recv()

    def take_left(packets, cs):
        for t in range(PG):
            put_columns(colv, 32 + cs * 3 + t, packets(t)[0:16, 512:640])
        rows = jnp.concatenate([packets(t) for t in range(PG)], axis=0)
        unpack_left(rows, winl, lscr, left, cs)

    def take_left_at(cs):
        take_left(lambda t: LF[cs, t], cs)

    def take_right(slots, cs):
        for slot in slots:
            put_columns(colv, slot * 8 + cs, RF[slot, cs, 0:16, 512:640])
        rows = jnp.concatenate([RF[slot, cs] for slot in slots], axis=0)
        unpack_right(rows, winr, compact, slots, cs)

    order = (2, 1, 3)
    for d in order:
        for ci in range(2):
            spread(d, ci).start()
    for t in range(3):
        cross(t).start()
    for ci in range(2):
        right_start(ci, 0)
    for d in order:
        left_own(d, col).start()
    for ci in range(2):
        right_relay(ci, 0)
    build_left_windows(winl)
    build_right_windows(winr)
    for n, d in enumerate(order):
        for ci in range(2):
            spread(d, ci).wait_recv()
            right_start(ci, d)
        for ci in range(2):
            if n:
                right_relay(ci, order[n - 1])
    for t in range(3):
        cross(t).wait_recv()
    for d in order:
        left_across(d, other + x).start()
    for ci in range(2):
        right_relay(ci, order[2])
    take_left(lambda t: F[(row + 2 * col + t) % 16], col)
    take_left(lambda t: LY[2 * x + t], other + x)

    def place(n):
        d = n // 2
        d = jnp.where(d == 0, 0, jnp.where(d == 1, order[0], jnp.where(d == 2, order[1], order[2])))
        h = jnp.where(n % 2 == 0, yh, 1 - yh)
        return h * 4 + (x + 4 - d) % 4

    def pairs(n, _):
        at = place(n)
        pair_arrived(at)
        hand(at).start()
        take_right((1, 2), at)
        return 0

    lax.fori_loop(0, 8, pairs, 0)
    for d in order:
        left_own(d, from_x(d)).wait_recv()
        take_left_at(from_x(d))

    def singles(n, _):
        at = place(n)
        single_arrived(at)
        handed(at)
        take_right((0, 3), at)
        return 0

    lax.fori_loop(0, 8, singles, 0)
    for d in order:
        at = other + (x + 4 - d) % 4
        left_across(d, at).wait_recv()
        take_left_at(at)
    for d in order:
        for ci in range(2):
            spread(d, ci).wait_send()
        left_own(d, col).wait_send()
        left_across(d, other + x).wait_send()
    for t in range(3):
        cross(t).wait_send()
    for ci in range(2):
        for d in range(4):
            right_sent(ci, d)
    for at in range(8):
        hand(at).wait_send()


def exchange(x_cols, x_blocks):
    unit = (ROWS, LANES)
    return pl.pallas_call(
        exchange_kernel,
        out_shape=[
            jax.ShapeDtypeStruct((56, 128), jnp.int32),
            jax.ShapeDtypeStruct((3, BB, KP, 256), BF16),
            jax.ShapeDtypeStruct((4, BB, PG, KP, 128), BF16),
        ],
        in_specs=[pl.BlockSpec(memory_space=pltpu.SMEM), pl.BlockSpec(memory_space=pltpu.VMEM)],
        out_specs=[pl.BlockSpec(memory_space=pltpu.VMEM)] * 3,
        scratch_shapes=[
            pltpu.VMEM((KEPT,) + unit, BF16),
            pltpu.VMEM((LANES // 128, (GROUPS + 1) * ROWS, 128), F32),
            pltpu.VMEM((2, 3, 2) + unit, BF16),
            pltpu.VMEM((9,) + unit, BF16),
            pltpu.VMEM((2, 4, 1) + unit, BF16),
            pltpu.VMEM((2, 4, 2) + unit, BF16),
            pltpu.VMEM((4, 8) + unit, BF16),
            pltpu.VMEM((8, 3) + unit, BF16),
            pltpu.VMEM((2 * PG, 2, KP + Q, 128), F32),
            pltpu.VMEM((RR, 256, 256), BF16),
            pltpu.VMEM(((RR + 1) // 2, 256, 256), BF16),
        ]
        + [DMA(shape) for shape in ((3, 2), (3,), (3,), (3,), (2, 2, 4)) for _ in range(2)]
        + [DMA((2, 2, 4))]
        + [DMA((8,)) for _ in range(5)],
        compiler_params=pltpu.CompilerParams(
            collective_id=0, has_side_effects=True, vmem_limit_bytes=40 << 20
        ),
        name="exchange",
    )(x_cols, x_blocks)


def expand(compact, dense, cols, slot, at, k):
    lane = lane_ids(KP)
    shift = 16 * BLK - 1024 if slot >= 2 else 0
    dense[at, k] = jnp.zeros((KP, WIDE), BF16)
    for p in range(PG):
        start = shift + BLK * cols[slot * 8 + k // 2, TAIL + (k % 2) * PG + p]
        t = start // 128
        d = start - 128 * t
        y = pltpu.roll(compact[slot, k, p], d, 1)
        zero = jnp.zeros_like(y)
        low = pl.ds(pl.multiple_of(128 * t, 128), 128)
        high = pl.ds(pl.multiple_of(128 * t + 128, 128), 128)
        dense[at, k, :, low] += jnp.where(lane >= d, y, zero)
        dense[at, k, :, high] += jnp.where(lane < d, y, zero)


def product_kernel(cols, left, compact, out, even, odd, total, osem):
    half = Q * BLK

    def rows_of(h, v, j):
        rows = 64 if v < Q - 1 else half - 64 * v
        lanes = pl.ds(0, 1024) if j == 0 else pl.ds(1024, 2 * BB * BLK - 1024)
        src = total.at[h, pl.ds(64 * v, rows), lanes]
        dst = out.at[pl.ds(pl.multiple_of(half * h + 64 * v, 8), rows), lanes]
        return pltpu.make_async_copy(src, dst, osem.at[j, Q * h + v])

    def first(n, _):
        for k in (2 * n, 2 * n + 1):
            for slot in range(2):
                expand(compact, even, cols, slot, slot, k)
        return 0

    lax.fori_loop(0, BB // 8, lambda n, _: [first(4 * n + v, 0) for v in range(4)][-1], 0)
    for h in range(2):
        total[h, 0:8, :] = jnp.zeros((8, total.shape[2]), F32)

    def multiply(h, v, j, dense):
        i = Q * h + v
        ls = [left[j + s, i][:, : PG * KP] for s in range(2)]
        ks = [
            [cols[32 + (i // 2) * 3 + j + s, TAIL + (i % 2) * PG + p] for p in range(PG)] for s in range(2)
        ]
        base = BLK * v // 8 * 8
        for n in range(5):
            acc = None
            for s in range(2):
                w = jnp.concatenate([dense[s, k, :, 256 * n : 256 * (n + 1)] for k in ks[s]], axis=0)
                term = jnp.dot(ls[s], w, preferred_element_type=F32)
                acc = term if acc is None else acc + term
            lo = 1024 * j + 256 * n
            width = min(256, total.shape[2] - lo)
            lanes = slice(lo, lo + width)
            if j == 1 and n == 0:
                total[h, base : base + 80, lanes] += acc
            else:
                total[h, base : base + 8, lanes] += acc[0:8, :width]
                total[h, base + 8 : base + 80, lanes] = acc[8:80, :width]

    def second(h, _):
        for v in range(Q):
            multiply(h, v, 0, even)
            for slot in range(2, 4):
                expand(compact, odd, cols, slot, slot - 2, Q * h + v)
            rows_of(h, v, 0).start()
        return 0

    lax.fori_loop(0, 2, second, 0)

    def third(h, _):
        for v in range(Q):
            multiply(h, v, 1, odd)
            rows_of(h, v, 1).start()
        return 0

    lax.fori_loop(0, 2, third, 0)
    for j in range(2):
        for h in range(2):
            for v in range(Q):
                rows_of(h, v, j).wait()


def product(cols, left, compact):
    return pl.pallas_call(
        product_kernel,
        out_shape=jax.ShapeDtypeStruct((BB * BLK, 2 * BB * BLK), F32),
        in_specs=[pl.BlockSpec(memory_space=pltpu.SMEM)] + [pl.BlockSpec(memory_space=pltpu.VMEM)] * 2,
        out_specs=pl.BlockSpec(memory_space=pl.ANY),
        scratch_shapes=[
            pltpu.VMEM((2, BB, KP, WIDE), BF16),
            pltpu.VMEM((2, BB, KP, WIDE), BF16),
            pltpu.VMEM((2, Q * BLK + 8, 2 * BB * BLK), F32),
            DMA((2, BB)),
        ],
        compiler_params=pltpu.CompilerParams(vmem_limit_bytes=36 << 20),
        name="product",
    )(cols, left, compact)


def shards(x_blocks, x_cols):
    cols, left, compact = exchange(
        x_cols.transpose(2, 0, 1), x_blocks.transpose(0, 2, 1, 3).reshape(2 * PG, GROUPS, SIZE)
    )
    return product(cols, left, compact)


def solution(mesh):
    in_specs = (P(("row", "col"), None, None, None), P(("row", "col"), None, None))
    return jax.shard_map(shards, mesh=mesh, in_specs=in_specs, out_specs=P("row", "col"), check_vma=False)
```
